256 devices in a mesh: elem: 64 (over z, y, core), gpt: 4 (over x).
Axes of the slice: x: 4, y: 4, z: 8, core: 2. Of those that a mesh axis runs over, the one named last changes fastest.
Arguments:
- thermal_state: float32 [72, 32768], P(None, 'elem'), may hold values from 0.7 to 1.3
- moisture_content: float32 [72, 32768], P(None, 'elem'), may hold values from 0.01 to 1
- lateral_velocity_components: float32 [2, 72, 32768], P(None, None, 'elem'), may hold values from -6 to 6
- sun_elevation_factor: float32 [32768], P('elem'), may hold values from 0.05 to 1
- surface_albedo_values: float32 [32768], P('elem'), may hold values from 0.1 to 0.9
- turbulent_diffusion_strength: float32 [32768], P('elem'), may hold values from 0.3 to 3
- sunlit_indicator: int32 [32768], P('elem'), may hold values 0 or 1
- destination_partition: int32 [32768, 1], P('elem'), may hold values from 0 to 63; in each aligned block of 512 rows (0 to 511, 512 to 1023, ...) at most 16 rows name the same one
- adjacent_elements: int32 [2048, 4], P('elem'), may hold values from 0 to 2047, as said below
- optical_extinction: float32 [56, 72], P('gpt'), may hold values from 0.002 to 0.05
- insolation_quadrature_share: float32 [56], P('gpt'), may hold values from 0.01 to 0.1
Outputs:
- tendency_out: float32 [4, 72, 32768], P(None, None, 'elem')
- span_heating: float32 [72, 65536], P(None, ('elem', 'gpt'))
The draws below stay inside these ranges and needn't reach their ends.
Inputs may be any that keep to these rules, and one draw needn't show every extreme that they name: `destination_partition`: among the 512 columns of one device at most 16 have the same span; in every draw some device has exactly 16 columns for one span. `adjacent_elements`: row e lists the elements e - 1, e + 1, e - a and e + b modulo 2048, with a and b from 1 to 32; b equals 32 for every element whose number is a multiple of 32.
All inputs are finite; a program needn't handle non-finite values. No bound on the sum of `sunlit_indicator` on one device may be relied on, other than what follows from the above.
Results may differ from the reference program's by a relative error of at most 0.000098.
Values sent between devices are 32-bit elements; how exact they have to be, the bound alone decides.
No kernel may reach another device: no remote copies, remote signals or barrier semaphores. Data moves between devices by JAX's collectives and lax.ppermute only.
A program may use at most 64 MiB of HBM per device.

```python
import math
import jax
import jax.numpy as jnp
import numpy as np
from jax import lax

LAYER_NUMBER = 72
BAND_QUADRATURE = 56
NF = 4
EPTS = 16
COL_DEV = 512
GRID_PROFILES = 32768
ELEM_DEV = 32
ELEMS = 2048
CAP = 16
SLOTS = 1024
N_ELEM = 64


def draw_adjacent_elements(key, part):
    first_key, second_key = jax.random.split(key)
    element = jnp.arange(ELEMS, dtype=jnp.int32)
    reach_back = jax.random.randint(first_key, (ELEMS,), 1, ELEM_DEV + 1, dtype=jnp.int32)
    reach_ahead = jax.random.randint(second_key, (ELEMS,), 1, ELEM_DEV + 1, dtype=jnp.int32)
    reach_ahead = jnp.where(element % ELEM_DEV == 0, ELEM_DEV, reach_ahead)
    listed = jnp.stack([(element - 1) % ELEMS, (element + 1) % ELEMS, (element - reach_back) % ELEMS, (element + reach_ahead) % ELEMS], axis=1)
    return listed.astype(jnp.int32)


def set_ends(result, rng, smallest, high):
    index_at = [jax.random.randint(jax.random.fold_in(rng, axis), (), 0, length) for axis, length in enumerate(result.shape)]
    main_axis = result.shape.index(max(result.shape))
    beside = index_at[:main_axis] + [(index_at[main_axis] + 1) % result.shape[main_axis]] + index_at[main_axis + 1:]
    return result.at[tuple(index_at)].set(smallest).at[tuple(beside)].set(high)


def shard_levels(key, dims, pieces, smallest, top_value):
    def one(axis_at, parts):
        heights = jax.random.uniform(jax.random.fold_in(jax.random.fold_in(key, 6), axis_at), (parts,), jnp.float32, smallest / len(pieces), top_value / len(pieces))
        return jnp.repeat(jnp.exp(heights), dims[axis_at] // parts).reshape((-1,) + (1,) * (len(dims) - axis_at - 1))

    loudness = one(*pieces[0])
    for cut in pieces[1:]:
        loudness = loudness * one(*cut)
    return loudness


def assign_block(rng, own, number, rows, count, top, most, skew):
    order = jax.random.permutation(rng, count)
    packed, usual = load_shares(count, rows * top, most, skew, True), load_shares(count, rows * top, most, skew, False)
    places = jnp.arange(count)

    def named(lengths, offset_by):
        used = int((lengths > 0).sum())
        fixed = max(1, used // 4)
        moved = fixed + (places - fixed + offset_by * (used - fixed)) % max(1, count - fixed)
        return jnp.zeros((count,), jnp.int32).at[order[jnp.where(places < fixed, places, moved)]].set(jnp.asarray(lengths, jnp.int32))

    lengths = jnp.where(number % 4 == 0, named(packed, number // 4), named(usual, number - number // 4 - 1))
    mixed = jax.random.permutation(jax.random.fold_in(own, 3), count)
    source_of, taker = mixed[0:count // 2 * 2:2], mixed[1:count // 2 * 2:2]
    margin = jnp.minimum(lengths[source_of] - 1, most - lengths[taker]) // 2
    margin = jnp.where((source_of == order[0]) | (taker == order[0]) | (lengths[taker] == 0), 0, jnp.maximum(margin, 0))
    moved = jax.random.randint(jax.random.fold_in(own, 4), (count // 2,), 0, 1 << 20) % (margin + 1)
    lengths = lengths.at[source_of].add(-moved).at[taker].add(moved)
    members = jnp.searchsorted(jnp.cumsum(lengths), jnp.arange(rows * top), side="right").astype(jnp.int32)
    table = members.reshape(top, rows).T
    table = table[jax.random.permutation(jax.random.fold_in(own, 1), rows)]
    offset_by = jax.random.randint(jax.random.fold_in(own, 2), (rows, 1), 0, top)
    return jnp.take_along_axis(table, (jnp.arange(top)[None, :] + offset_by) % top, axis=1)


def load_shares(amount, total, reach, lean, full):
    portions = [(1 << 20) // math.isqrt(standing ** lean) + 1 for standing in range(1, amount + 1)]
    largest = reach if full else min(reach, max(-(-total // amount), total * portions[0] // sum(portions)))
    least = 1 if total - largest >= amount - 1 else 0
    given, rest = [largest] + [least] * (amount - 1), total - largest - least * (amount - 1)
    while rest > 0:
        free = [i for i in range(1, amount) if given[i] < largest] or [i for i in range(1, amount) if given[i] < reach]
        whole, budget = sum([portions[i] for i in free]), rest
        for i in free:
            extra = min(reach - given[i], max(1, budget * portions[i] // whole), rest)
            given[i] = given[i] + extra
            rest = rest - extra
    return np.array(given)


def scatter_about(rng, dims, deviation, bound, pieces=(), kind=jnp.bfloat16):
    array = jax.random.normal(rng, dims, jnp.float32) * deviation
    if len(pieces) > 0:
        array = shard_levels(rng, dims, pieces, -0.22, 0.18) * array
    return jnp.clip(array, min=-bound, max=bound).astype(kind)


def setup_inputs(seed: int = 0) -> dict:
    arg_keys = jax.random.split(jax.random.key(seed), 12)
    thermal_state = jnp.clip(0.7 + 0.59999996 * jax.random.uniform(arg_keys[0], (LAYER_NUMBER, GRID_PROFILES), jnp.float32) ** shard_levels(arg_keys[0], (LAYER_NUMBER, GRID_PROFILES), ((1, 64),), -0.2, 0.2), 0.7, 1.3)
    moisture_content = jnp.clip(jnp.exp(math.log(1.0) - 4.6051702 * jax.random.uniform(arg_keys[1], (LAYER_NUMBER, GRID_PROFILES), jnp.float32) ** shard_levels(arg_keys[1], (LAYER_NUMBER, GRID_PROFILES), ((1, 64),), -0.2, 0.2)), 0.01, 1.0)
    lateral_velocity_components = scatter_about(arg_keys[2], (2, LAYER_NUMBER, GRID_PROFILES), 1.0, 6.0, ((2, 64),), jnp.float32)
    sun_elevation_factor = jnp.clip(jnp.exp(math.log(1.0) - 2.9957323 * jax.random.uniform(arg_keys[3], (GRID_PROFILES,), jnp.float32) ** shard_levels(arg_keys[3], (GRID_PROFILES,), ((0, 64),), -0.2, 0.2)), 0.05, 1.0)
    surface_albedo_values = jnp.clip(0.1 + 0.79999997 * jax.random.uniform(arg_keys[4], (GRID_PROFILES,), jnp.float32) ** shard_levels(arg_keys[4], (GRID_PROFILES,), ((0, 64),), -0.2, 0.2), 0.1, 0.9)
    turbulent_diffusion_strength = jnp.clip(jnp.exp(math.log(3.0) - 2.3025851 * jax.random.uniform(arg_keys[5], (GRID_PROFILES,), jnp.float32) ** shard_levels(arg_keys[5], (GRID_PROFILES,), ((0, 64),), -0.2, 0.2)), 0.3, 3.0)
    sunlit_indicator = set_ends((jax.random.randint(arg_keys[6], (GRID_PROFILES,), 0, 2) < 1).astype(jnp.int32), jax.random.fold_in(arg_keys[6], 1), 0, 1)
    destination_partition_keys = jax.random.split(jax.random.fold_in(arg_keys[7], 1), GRID_PROFILES // COL_DEV)
    destination_partition_turns = jax.random.permutation(jax.random.fold_in(arg_keys[7], 3), GRID_PROFILES // COL_DEV)
    destination_partition = jax.vmap(lambda own, number: assign_block(jax.random.fold_in(arg_keys[7], 2), own, number, COL_DEV, N_ELEM, 1, CAP, 2))(destination_partition_keys, destination_partition_turns).reshape((GRID_PROFILES, 1))
    adjacent_elements = draw_adjacent_elements(jax.random.fold_in(arg_keys[11], 71), 0)
    optical_extinction = jnp.clip(jnp.exp(math.log(0.05) - 3.218876 * jax.random.uniform(arg_keys[9], (BAND_QUADRATURE, LAYER_NUMBER), jnp.float32) ** shard_levels(arg_keys[9], (BAND_QUADRATURE, LAYER_NUMBER), ((0, 4),), -0.2, 0.2)), 0.002, 0.05)
    insolation_quadrature_share = jnp.clip(jnp.exp(math.log(0.1) - 2.3025851 * jax.random.uniform(arg_keys[10], (BAND_QUADRATURE,), jnp.float32) ** shard_levels(arg_keys[10], (BAND_QUADRATURE,), ((0, 4),), -0.2, 0.2)), 0.01, 0.1)
    return dict(thermal_state=thermal_state, moisture_content=moisture_content, lateral_velocity_components=lateral_velocity_components, sun_elevation_factor=sun_elevation_factor, surface_albedo_values=surface_albedo_values, turbulent_diffusion_strength=turbulent_diffusion_strength, sunlit_indicator=sunlit_indicator, destination_partition=destination_partition, adjacent_elements=adjacent_elements, optical_extinction=optical_extinction, insolation_quadrature_share=insolation_quadrature_share)


diffusivity = 1.66
coupling = 0.5


def thomas_solve(right_side, upper_coef, lower_coef):
    def forward_sweep(carried, inputs):
        ratio_prev, value_prev = carried
        side_now, upper_now, lower_now = inputs
        denominator = 1.0 + upper_now + lower_now - upper_now * ratio_prev
        ratio_now = lower_now / denominator
        value_now = (side_now + upper_now * value_prev) / denominator
        return (ratio_now, value_now), (ratio_now, value_now)

    start = jnp.zeros_like(right_side[0])
    unused, (ratios, values) = lax.scan(forward_sweep, (start, start), (right_side, upper_coef, lower_coef))

    def backward_sweep(carried, inputs):
        ratio_now, value_now = inputs
        solved = value_now + ratio_now * carried
        return solved, solved

    unused, solved = lax.scan(backward_sweep, start, (ratios, values), reverse=True)
    return solved


def sunlight_warming(thermal_state, moisture_content, overhead_angle_factor, albedo_factor, optical_extinction, insolation_quadrature_share):
    irradiance_times_absorbed = moisture_content * thermal_state

    def spectral_quadrature_point(gpoint, heating_totals):
        depths = optical_extinction[gpoint][:, None] * irradiance_times_absorbed
        below_sum = jnp.cumsum(depths, axis=0)
        above_sum = below_sum - depths
        column_total = below_sum[-1:]
        downward = jnp.exp(-above_sum / overhead_angle_factor) - jnp.exp(-below_sum / overhead_angle_factor)
        surface = albedo_factor * jnp.exp(-column_total / overhead_angle_factor)
        upward = surface * (jnp.exp(-diffusivity * (column_total - below_sum)) - jnp.exp(-diffusivity * (column_total - above_sum)))
        return heating_totals + insolation_quadrature_share[gpoint] * (downward + upward)

    return lax.fori_loop(0, BAND_QUADRATURE, spectral_quadrature_point, jnp.zeros_like(thermal_state))


def reference(thermal_state, moisture_content, lateral_velocity_components, sun_elevation_factor, surface_albedo_values, turbulent_diffusion_strength, sunlit_indicator, destination_partition, adjacent_elements, optical_extinction, insolation_quadrature_share):
    warming_tendency = sunlight_warming(thermal_state, moisture_content, sun_elevation_factor, surface_albedo_values, optical_extinction, insolation_quadrature_share) * sunlit_indicator.astype(jnp.float32)
    present_variables = jnp.concatenate([thermal_state[None], moisture_content[None], lateral_velocity_components], axis=0)
    right_side = present_variables.at[0].add(warming_tendency)
    shear_sum = jnp.sum((lateral_velocity_components[:, :-1] - lateral_velocity_components[:, 1:]) ** 2, axis=0)
    interface_mix = turbulent_diffusion_strength * (1.0 + shear_sum)
    zero_row = jnp.zeros_like(interface_mix[:1])
    upper_coef = jnp.concatenate([zero_row, interface_mix], axis=0)[:, None]
    lower_coef = jnp.concatenate([interface_mix, zero_row], axis=0)[:, None]
    solved = thomas_solve(jnp.transpose(right_side, (1, 0, 2)), upper_coef, lower_coef)
    tendency = jnp.transpose(solved, (1, 0, 2)) - present_variables
    grouped = tendency.reshape(NF, LAYER_NUMBER, ELEMS, EPTS)
    averages = jnp.mean(grouped, axis=-1)
    beside = jnp.sum(averages[:, :, adjacent_elements], axis=-1)
    corrected = grouped + coupling * (beside - 4.0 * averages)[..., None]
    tendency_out = corrected.reshape(NF, LAYER_NUMBER, GRID_PROFILES)
    targets = destination_partition[:, 0].reshape(N_ELEM, COL_DEV)
    onehot = (targets[:, :, None] == jnp.arange(N_ELEM, dtype=jnp.int32)[None, None, :]).astype(jnp.int32)
    ranking = jnp.sum(jnp.cumsum(onehot, axis=1) * onehot, axis=-1) - 1
    sources = jnp.arange(N_ELEM, dtype=jnp.int32)[:, None]
    position = (targets * SLOTS + sources * CAP + ranking).reshape(GRID_PROFILES).astype(jnp.int32)
    span_heating = jnp.zeros((LAYER_NUMBER, N_ELEM * SLOTS), jnp.float32).at[:, position].set(warming_tendency)
    return tendency_out, span_heating
```

```python
import functools
import math

import jax
import jax.numpy as jnp
from jax import lax
from jax.experimental import pallas as pl
from jax.experimental.pallas import tpu as pltpu
from jax.sharding import PartitionSpec as P

LEVELS = 72
COLS = 512
EPTS = 16
LANES = 128
GROUPS = 7
DIFFUSIVITY = 1.66
SCALE = DIFFUSIVITY * math.log2(math.e)
VMEM = pl.BlockSpec(memory_space=pltpu.VMEM)
AXES = ("elem", "gpt")
BF16 = jnp.bfloat16
F32 = jnp.float32


def iota(shape, dim):
    return lax.broadcasted_iota(jnp.int32, shape, dim)


def split(x):
    high = x.astype(BF16)
    rest = x - high.astype(F32)
    middle = rest.astype(BF16)
    low = (rest - middle.astype(F32)).astype(BF16)
    return jnp.concatenate([high, middle, low], axis=0)


def joined(y):
    rows = y.shape[0] // 3
    return y[:rows] + y[rows : 2 * rows] + y[2 * rows :]


def times(x, table):
    return joined(jnp.dot(split(x), table, preferred_element_type=F32))


def element_mean(field):
    at = field * 32 + (iota((COLS, LANES), 0) >> 4)
    return jnp.where(iota((COLS, LANES), 1) == at, 1.0 / EPTS, 0.0).astype(BF16)


def pack_kernel(t_ref, q_ref, mu_ref, albedo_ref, lit_ref, dest_ref, *outs):
    place = lax.axis_index("elem") & 15
    member = lax.axis_index("gpt")
    dest = dest_ref[...]
    onehot = jnp.where(dest == iota((64, COLS), 0), 1.0, 0.0)
    before = jnp.where(iota((COLS, COLS), 0) < iota((COLS, COLS), 1), 1.0, 0.0).astype(BF16)
    earlier = jnp.dot(onehot.astype(BF16), before, preferred_element_type=F32)
    rank = jnp.sum(onehot * earlier, axis=0, keepdims=True).astype(jnp.int32)
    apart = (dest & 15) ^ place
    slot = (apart & 3) * 64 + (apart >> 2) * 16 + rank
    sent = ((dest >> 4) == member) & (lit_ref[...] != 0)
    slot = jnp.where(sent, slot, -1)
    chosen = jnp.where(slot == iota((256, COLS), 0), 1.0, 0.0).astype(BF16)
    row = iota((8, COLS), 0)
    tail = jnp.where(row == 0, mu_ref[...], jnp.where(row == 1, albedo_ref[...], 0.0))
    table = jnp.concatenate([t_ref[...] * q_ref[...], tail], axis=0)
    packed = joined(
        lax.dot_general(
            split(table), chosen, (((1,), (1,)), ((), ())), preferred_element_type=F32
        )
    )
    for r, out in enumerate(outs):
        part = packed[:, 64 * r : 64 * r + 64]
        out[...] = jnp.concatenate([part[:40], part[40:]], axis=1)


def regroup_kernel(*refs):
    group = (iota((40, LANES), 1) >> 4) & 3
    for q in range(4):
        out = jnp.zeros((40, LANES), F32)
        for r in range(4):
            moved = refs[r][...]
            if r != q:
                moved = pltpu.roll(moved, (16 * (r - q)) % LANES, 1)
            out = jnp.where(group == r, moved, out)
        refs[4 + q][...] = out


def heat_columns(a_ref, heat_ref, ext_ref, weight_ref, surface_ref, mu, albedo, tiles):
    columns = a_ref.shape[1]
    slope = -1.0 / (DIFFUSIVITY * mu)
    total = jnp.dot(
        ext_ref[:, :LEVELS],
        a_ref[:LEVELS, :],
        precision=lax.Precision.HIGHEST,
        preferred_element_type=F32,
    )
    weight_ref[...] = jnp.broadcast_to(ext_ref[:, LEVELS : LEVELS + 1] * (1.0 / SCALE), (56, LANES))
    for tile in range(columns // LANES):
        at = slice(LANES * tile, LANES * tile + LANES)
        surface_ref[:, at] = (
            weight_ref[...] * albedo[:, at] * jnp.exp2(total[:, at] * (slope[:, at] - 1.0))
        )
    for first in range(0, columns // LANES, tiles):
        spans = [slice(LANES * t, LANES * t + LANES) for t in range(first, first + tiles)]
        slopes = [jnp.broadcast_to(slope[:, at], (8, LANES)) for at in spans]
        start = []
        for at in spans:
            flux = jnp.zeros((8, LANES), F32)
            for o in range(GROUPS):
                flux = flux + (weight_ref[8 * o : 8 * o + 8] - surface_ref[8 * o : 8 * o + 8, at])
            start.append(flux)

        def step(octet, carried, spans=spans, slopes=slopes):
            exts, depths, fluxes = carried
            depths, fluxes = [list(d) for d in depths], list(fluxes)
            base = pl.ds(pl.multiple_of(octet * 8, 8), 8)
            arrays = [a_ref[base, at] for at in spans]
            heats = [[] for _ in spans]
            for s in range(8):
                rows = [jnp.broadcast_to(a[s : s + 1], (8, LANES)) for a in arrays]
                now = [None] * tiles
                for o in range(GROUPS):
                    ext = jnp.broadcast_to(exts[o][:, s : s + 1], (8, LANES))
                    weight = weight_ref[8 * o : 8 * o + 8]
                    for t in range(tiles):
                        depth = depths[o][t] + ext * rows[t]
                        depths[o][t] = depth
                        flux = weight * jnp.exp2(depth * slopes[t]) - surface_ref[
                            8 * o : 8 * o + 8, spans[t]
                        ] * jnp.exp2(depth)
                        now[t] = flux if now[t] is None else now[t] + flux
                for t in range(tiles):
                    heats[t].append(jnp.sum(fluxes[t] - now[t], axis=0, keepdims=True))
                    fluxes[t] = now[t]
            for t in range(tiles):
                heat_ref[base, spans[t]] = jnp.concatenate(heats[t], axis=0)
            exts = [pltpu.roll(e, LANES - 8, 1) for e in exts]
            return exts, depths, fluxes

        zero = jnp.zeros((8, LANES), F32)
        lax.fori_loop(
            0,
            LEVELS // 8,
            step,
            (
                [ext_ref[8 * o : 8 * o + 8] for o in range(GROUPS)],
                [[zero] * tiles for _ in range(GROUPS)],
                start,
            ),
        )


def load_extinction(blocks, ext_ref):
    for k, block in enumerate(blocks):
        ext_ref[14 * k : 14 * k + 14] = block[:14] * SCALE


def octet(count):
    return pl.ds(pl.multiple_of(count * 8, 8), 8)


def spread_row(block, s):
    return jnp.broadcast_to(block[s : s + 1], block.shape)


def sweep(arrays, step, carried, backward=False):
    reads, writes = arrays
    sublane = iota((8, COLS), 0)

    def body(count, carried):
        at = octet(LEVELS // 8 - 1 - count if backward else count)
        blocks = [read(at) for read in reads]
        kept = [None] * len(writes)
        for s in reversed(range(8)) if backward else range(8):
            carried, results = step(carried, *[spread_row(b, s) for b in blocks])
            kept = [r if k is None else jnp.where(sublane == s, r, k) for k, r in zip(kept, results)]
        for write, k in zip(writes, kept):
            write(at, k)
        return carried

    lax.fori_loop(0, LEVELS // 8, body, carried)


def reader(ref, *first):
    return lambda at: ref[(*first, at, slice(None))]


def writer(ref, *first):
    def write(at, value):
        ref[(*first, at, slice(None))] = value

    return write


def factor_kernel(
    q_ref, wind_ref, strength_ref, adjacent_ref,
    inv_ref, down_ref, ratio_ref, tend_ref, avg_ref, correct_ref,
    upper_ref, lower_ref, value_ref,
):
    u, v = wind_ref[0], wind_ref[1]
    mix = strength_ref[...] * (1.0 + ((u[:-1] - u[1:]) ** 2 + (v[:-1] - v[1:]) ** 2))
    edge = jnp.zeros((1, COLS), F32)
    upper_ref[...] = jnp.concatenate([edge, mix], axis=0)
    lower_ref[...] = jnp.concatenate([mix, edge], axis=0)

    def forward(carried, upper, lower, *sides):
        ratio, values = carried
        inverse = 1.0 / ((1.0 + upper + lower) - upper * ratio)
        ratio = lower * inverse
        down = upper * inverse
        values = [side * inverse + down * value for side, value in zip(sides, values)]
        return (ratio, values), (inverse, down, ratio, *values)

    zero = jnp.zeros((8, COLS), F32)
    sides = [reader(q_ref), reader(wind_ref, 0), reader(wind_ref, 1)]
    sweep(
        (
            [reader(upper_ref), reader(lower_ref), *sides],
            [writer(inv_ref), writer(down_ref), writer(ratio_ref)]
            + [writer(value_ref, f) for f in range(3)],
        ),
        forward,
        (zero, [zero] * 3),
    )

    def backward(solved, ratio, *values):
        solved = [value + ratio * x for value, x in zip(values, solved)]
        return solved, solved

    sweep(
        (
            [reader(ratio_ref)] + [reader(value_ref, f) for f in range(3)],
            [writer(value_ref, f) for f in range(3)],
        ),
        backward,
        [zero] * 3,
        True,
    )
    tend_ref[0] = value_ref[0] - q_ref[...]
    tend_ref[1:3] = value_ref[1:3] - wind_ref[...]
    avg = jnp.zeros((LEVELS, LANES), F32)
    for f in range(3):
        avg = avg + times(tend_ref[f], element_mean(f + 1))
    avg_ref[...] = avg
    first = lax.axis_index("elem") * 32
    local = (adjacent_ref[...] - first + 32) & 2047
    spread = jnp.where(iota((32, COLS), 0) == (iota((32, COLS), 1) >> 4), 1.0, 0.0).astype(BF16)
    local = jnp.dot(
        local.astype(F32).astype(BF16), spread, preferred_element_type=F32
    ).astype(jnp.int32)
    row = iota((LANES, COLS), 0)
    weight = jnp.where(row == 32 + (iota((LANES, COLS), 1) >> 4), -2.0, 0.0)
    for k in range(4):
        weight = weight + jnp.where(row == local[k : k + 1], 0.5, 0.0)
    correct_ref[...] = weight.astype(BF16)


def home_kernel(
    e0, e1, e2, e3, t_ref, q_ref, mu_ref, albedo_ref, lit_ref, inv_ref, down_ref, ratio_ref, early_ref,
    tend_ref, avg_ref,
    a_ref, heat_ref, ext_ref, weight_ref, surface_ref,
):
    load_extinction((e0, e1, e2, e3), ext_ref)
    a_ref[...] = t_ref[...] * q_ref[...]
    heat_columns(
        a_ref, heat_ref, ext_ref, weight_ref, surface_ref, mu_ref[...], albedo_ref[...], 2
    )
    side = t_ref[...] + heat_ref[...] * lit_ref[...].astype(F32)
    heat_ref[...] = side * inv_ref[...]


    def forward(value, side, down):
        value = side + down * value
        return value, (value,)

    def backward(solved, value, ratio):
        solved = value + ratio * solved
        return solved, (solved,)

    zero = jnp.zeros((8, COLS), F32)
    writes = [writer(heat_ref)]
    sweep(([reader(heat_ref), reader(down_ref)], writes), forward, zero)
    sweep(([reader(heat_ref), reader(ratio_ref)], writes), backward, zero, True)
    tend = heat_ref[...] - t_ref[...]
    tend_ref[...] = tend
    avg_ref[...] = early_ref[...] + times(tend, element_mean(0))


def span_kernel(
    e0, e1, e2, e3, m0, m1, m2, m3,
    out_ref,
    a_ref, heat_ref, ext_ref, weight_ref, surface_ref,
):
    load_extinction((e0, e1, e2, e3), ext_ref)
    low_half = iota((40, LANES), 1) < 64
    for tile, (a, b) in enumerate(((m0, m1), (m2, m3))):
        a, b = a[...], b[...]
        at = slice(LANES * tile, LANES * tile + LANES)
        a_ref[0:40, at] = jnp.where(low_half, a, pltpu.roll(b, 64, 1))
        a_ref[40:80, at] = jnp.where(low_half, pltpu.roll(a, 64, 1), b)
    mu = a_ref[LEVELS : LEVELS + 1, :]
    albedo = a_ref[LEVELS + 1 : LEVELS + 2, :]
    occupied = mu > 0.0
    heat_columns(
        a_ref, heat_ref, ext_ref, weight_ref, surface_ref, jnp.where(occupied, mu, 1.0), albedo, 2
    )
    place = lax.axis_index("elem") & 15
    heat = jnp.where(occupied, heat_ref[...], 0.0)
    parts = [heat[:, :LANES], heat[:, LANES:]]
    group = iota((LEVELS, LANES), 1) >> 4
    for k in range(3):
        width = 16 << k
        turn = ((place >> k) & 1) == 1
        parts = [
            jnp.where(
                turn,
                jnp.where(
                    ((group >> k) & 1) == 0,
                    pltpu.roll(x, LANES - width, 1),
                    pltpu.roll(x, width, 1),
                ),
                x,
            )
            for x in parts
        ]
    turn = (place >> 3) == 1
    out_ref[:, :LANES] = jnp.where(turn, parts[1], parts[0])
    out_ref[:, LANES:] = jnp.where(turn, parts[0], parts[1])


def finish_kernel(tend0_ref, tend_ref, avg_ref, left_ref, right_ref, correct_ref, out_ref):
    lane = iota((LEVELS, LANES), 1)
    left, own, right = left_ref[...], avg_ref[...], right_ref[...]
    table = correct_ref[...]

    def turned(x, by):
        by = by % LANES
        return pltpu.roll(x, by, 1) if by else x

    for f in range(4):
        wide = jnp.where(
            lane < 32,
            turned(left, -32 * f),
            jnp.where(lane < 64, turned(own, 32 - 32 * f), turned(right, 64 - 32 * f)),
        )
        wide = jnp.where(lane < 96, wide, 0.0)
        tend = tend0_ref[...] if f == 0 else tend_ref[f - 1]
        out_ref[f] = tend + times(wide, table)


def call(kernel, outs, scratch, *args):
    return pl.pallas_call(
        kernel,
        out_shape=outs,
        in_specs=[VMEM] * len(args),
        out_specs=jax.tree.map(lambda _: VMEM, outs),
        scratch_shapes=scratch,
        compiler_params=pltpu.CompilerParams(vmem_limit_bytes=32 * 1024 * 1024),
    )(*args)


def shape(*dims, dtype=F32):
    return jax.ShapeDtypeStruct(dims, dtype)


def number(s, m):
    return 4 * s + m


STAGE_ONE = [
    [(number(s, m), number(s ^ r, m)) for s in range(64) for m in range(4)] for r in range(4)
]
STAGE_TWO = [
    [
        (number(16 * g + i, m), number(16 * m + (i ^ (4 * q)), g))
        for g in range(4)
        for i in range(16)
        for m in range(4)
    ]
    for q in range(4)
]
ROUND = [[(k, (k + step) % 4) for k in range(4)] for step in range(4)]
UP = [(k, (k + 1) % 64) for k in range(64)]
DOWN = [(b, a) for a, b in UP]


def shards(
    thermal_state,
    moisture_content,
    lateral_velocity_components,
    sun_elevation_factor,
    surface_albedo_values,
    turbulent_diffusion_strength,
    sunlit_indicator,
    destination_partition,
    adjacent_elements,
    optical_extinction,
    insolation_quadrature_share,
):
    row = lambda x: x.reshape(1, COLS)
    mu, albedo = row(sun_elevation_factor), row(surface_albedo_values)
    lit, strength = row(sunlit_indicator), row(turbulent_diffusion_strength)
    own_ext = jnp.pad(
        jnp.concatenate([optical_extinction, insolation_quadrature_share[:, None]], axis=1),
        ((0, 2), (0, LANES - LEVELS - 1)),
    )
    exts = [own_ext] + [lax.ppermute(own_ext, "gpt", ROUND[k]) for k in (1, 2, 3)]
    field = shape(LEVELS, COLS)
    block = shape(40, LANES)
    packed = call(
        pack_kernel,
        [block] * 4,
        [],
        thermal_state,
        moisture_content,
        mu,
        albedo,
        lit,
        row(destination_partition),
    )
    gathered = [packed[0]] + [lax.ppermute(packed[r], AXES, STAGE_ONE[r]) for r in (1, 2, 3)]
    inverse, down, ratio, tend_late, early, correct = call(
        factor_kernel,
        [
            field, field, field, shape(3, LEVELS, COLS), shape(LEVELS, LANES),
            shape(LANES, COLS, dtype=BF16),
        ],
        [pltpu.VMEM((LEVELS, COLS), F32)] * 2 + [pltpu.VMEM((3, LEVELS, COLS), F32)],
        moisture_content,
        lateral_velocity_components,
        strength,
        adjacent_elements.T,
    )
    regrouped = call(regroup_kernel, [block] * 4, [], *gathered)
    arrived = [lax.ppermute(regrouped[q], AXES, STAGE_TWO[q]) for q in range(4)]

    def work(columns, rows):
        return [
            pltpu.VMEM((rows, columns), F32),
            pltpu.VMEM((LEVELS, columns), F32),
            pltpu.VMEM((56, LANES), F32),
            pltpu.VMEM((56, LANES), F32),
            pltpu.VMEM((56, columns), F32),
        ]

    tend0, average = call(
        home_kernel,
        [field, shape(LEVELS, LANES)],
        work(COLS, LEVELS),
        *exts, thermal_state, moisture_content, mu, albedo, lit, inverse, down, ratio, early,
    )
    left = lax.ppermute(average, "elem", UP)
    right = lax.ppermute(average, "elem", DOWN)
    span_heating = call(span_kernel, shape(LEVELS, 256), work(256, 80), *exts, *arrived)
    tendency_out = call(
        finish_kernel, shape(4, LEVELS, COLS), [], tend0, tend_late, average, left, right, correct
    )
    return tendency_out, span_heating


def solution(mesh):
    return jax.shard_map(
        shards,
        mesh=mesh,
        in_specs=(
            P(None, "elem"),
            P(None, "elem"),
            P(None, None, "elem"),
            P("elem"),
            P("elem"),
            P("elem"),
            P("elem"),
            P("elem", None),
            P("elem", None),
            P("gpt", None),
            P("gpt"),
        ),
        out_specs=(P(None, None, "elem"), P(None, ("elem", "gpt"))),
        check_vma=False,
    )
```

```python
import functools
import math

import jax
import jax.numpy as jnp
from jax import lax
from jax.experimental import pallas as pl
from jax.experimental.pallas import tpu as pltpu
from jax.sharding import PartitionSpec as P

LEVELS = 72
COLS = 512
EPTS = 16
LANES = 128
WIDE = 1280
GROUPS = 7
DIFFUSIVITY = 1.66
SCALE = DIFFUSIVITY * math.log2(math.e)
VMEM = pl.BlockSpec(memory_space=pltpu.VMEM)
AXES = ("elem", "gpt")
BF16 = jnp.bfloat16
F32 = jnp.float32


def iota(shape, dim):
    return lax.broadcasted_iota(jnp.int32, shape, dim)


def split(x):
    high = x.astype(BF16)
    rest = x - high.astype(F32)
    middle = rest.astype(BF16)
    low = (rest - middle.astype(F32)).astype(BF16)
    return jnp.concatenate([high, middle, low], axis=0)


def joined(y):
    rows = y.shape[0] // 3
    return y[:rows] + y[rows : 2 * rows] + y[2 * rows :]


def times(x, table):
    return joined(jnp.dot(split(x), table, preferred_element_type=F32))


def element_mean(field):
    at = field * 32 + (iota((COLS, LANES), 0) >> 4)
    return jnp.where(iota((COLS, LANES), 1) == at, 1.0 / EPTS, 0.0).astype(BF16)


def swap_groups(x):
    sublane, group = iota((8, LANES), 0), iota((8, LANES), 1) >> 4
    for k in range(3):
        height, width = 1 << k, 16 << k
        up = pltpu.roll(pltpu.roll(x, 8 - height, 0), width, 1)
        down = pltpu.roll(pltpu.roll(x, height, 0), LANES - width, 1)
        in_row, in_lane = (sublane >> k) & 1, (group >> k) & 1
        x = jnp.where(in_row == in_lane, x, jnp.where(in_row == 0, up, down))
    return x


STRENGTH, LIT, ADJACENT, MU, ALBEDO = 0, 1, 2, 6, 7


def pack_kernel(
    t_ref, q_ref, mu_ref, albedo_ref, lit_ref, dest_ref, strength_ref, adjacent_ref,
    low_ref, high_ref, scalar_ref,
):
    scalar_ref[STRENGTH : STRENGTH + 1] = strength_ref[...]
    scalar_ref[LIT : LIT + 1] = lit_ref[...].astype(F32)
    scalar_ref[ADJACENT:MU, :32] = adjacent_ref[...].astype(F32)
    scalar_ref[MU : MU + 1] = mu_ref[...]
    scalar_ref[ALBEDO : ALBEDO + 1] = albedo_ref[...]
    served = (2 * (lax.axis_index("elem") >> 4) + 2 - lax.axis_index("gpt")) & 3
    before = jnp.where(iota((LANES, LANES), 0) < iota((LANES, LANES), 1), 1.0, 0.0).astype(BF16)
    dest = dest_ref[...]
    number_of = iota((64, LANES), 0)
    gone = jnp.zeros((64, 1), F32)
    ranks = []
    for tile in range(COLS // LANES):
        onehot = jnp.where(dest[:, LANES * tile : LANES * tile + LANES] == number_of, 1.0, 0.0)
        earlier = jnp.dot(onehot.astype(BF16), before, preferred_element_type=F32)
        ranks.append(jnp.sum(onehot * (earlier + gone), axis=0, keepdims=True))
        gone = gone + jnp.sum(onehot, axis=1, keepdims=True)
    rank = jnp.concatenate(ranks, axis=1).astype(jnp.int32)
    sent = ((dest >> 4) == served) & (lit_ref[...] != 0)
    apart = (dest ^ lax.axis_index("elem")) & 15
    slot = jnp.where(sent, apart * 16 + rank, -1)
    chosen = jnp.where(slot == iota((256, COLS), 0), 1.0, 0.0).astype(BF16)
    row = iota((8, COLS), 0)
    tail = jnp.where(row == 0, mu_ref[...], jnp.where(row == 1, albedo_ref[...], 0.0))
    table = jnp.concatenate([t_ref[...] * q_ref[...], tail], axis=0)
    packed = joined(
        lax.dot_general(
            split(table), chosen, (((1,), (1,)), ((), ())), preferred_element_type=F32
        )
    )
    for half, out_ref in enumerate((low_ref, high_ref)):
        for o in range(10):
            part = packed[8 * o : 8 * o + 8, LANES * half : LANES * half + LANES]
            at = slice(LANES * o, LANES * o + LANES)
            out_ref[:, at] = swap_groups(part)


def bit_of_row(bit):
    return (iota((8, WIDE), 0) >> bit) & 1


def taken(low, high, bit):
    return jnp.where(bit_of_row(bit) == 0, pltpu.roll(low, 8 - (1 << bit), 0), high)


def put(low, high, got, bit):
    clear = bit_of_row(bit) == 0
    return jnp.where(clear, low, pltpu.roll(got, 1 << bit, 0)), jnp.where(clear, high, got)


def held(blocks):
    low, high = blocks[0][...], blocks[1][...]
    for bit, got in zip((2, 1, 0), blocks[2:]):
        low, high = put(low, high, got[...], bit)
    return low, high


def pair_kernel(own_ref, beside_ref, exts_ref):
    exts_ref[:16] = own_ref[...]
    exts_ref[16:] = beside_ref[...]


def next_kernel(*refs):
    *blocks, out_ref = refs
    low, high = held(blocks)
    out_ref[...] = taken(low, high, 4 - len(blocks))


def last_kernel(b0, b1, b2, b3, avg_ref, out_ref):
    low, high = held((b0, b1, b2, b3))
    out_ref[:, :WIDE] = taken(low, high, 0)
    for o in range(LEVELS // 8):
        out_ref[:, WIDE + LANES * o : WIDE + LANES * o + LANES] = avg_ref[8 * o : 8 * o + 8]


def heat_columns(a_ref, heat_ref, ext_ref, weight_ref, surface_ref, mu, albedo, tiles):
    columns = a_ref.shape[1]
    slope = -1.0 / (DIFFUSIVITY * mu)
    total = jnp.dot(
        ext_ref[:, :LEVELS],
        a_ref[:LEVELS, :],
        precision=lax.Precision.HIGHEST,
        preferred_element_type=F32,
    )
    weight_ref[...] = jnp.broadcast_to(ext_ref[:, LEVELS : LEVELS + 1] * (1.0 / SCALE), (56, LANES))
    for tile in range(columns // LANES):
        at = slice(LANES * tile, LANES * tile + LANES)
        surface_ref[:, at] = (
            weight_ref[...] * albedo[:, at] * jnp.exp2(total[:, at] * (slope[:, at] - 1.0))
        )
    for first in range(0, columns // LANES, tiles):
        spans = [slice(LANES * t, LANES * t + LANES) for t in range(first, first + tiles)]
        slopes = [jnp.broadcast_to(slope[:, at], (8, LANES)) for at in spans]
        start = []
        for at in spans:
            flux = jnp.zeros((8, LANES), F32)
            for o in range(GROUPS):
                flux = flux + (weight_ref[8 * o : 8 * o + 8] - surface_ref[8 * o : 8 * o + 8, at])
            start.append(flux)

        def step(octet, carried, spans=spans, slopes=slopes):
            exts, depths, fluxes = carried
            depths, fluxes = [list(d) for d in depths], list(fluxes)
            base = pl.ds(pl.multiple_of(octet * 8, 8), 8)
            arrays = [a_ref[base, at] for at in spans]
            heats = [[] for _ in spans]
            for s in range(8):
                rows = [jnp.broadcast_to(a[s : s + 1], (8, LANES)) for a in arrays]
                now = [None] * tiles
                for o in range(GROUPS):
                    ext = jnp.broadcast_to(exts[o][:, s : s + 1], (8, LANES))
                    weight = weight_ref[8 * o : 8 * o + 8]
                    for t in range(tiles):
                        depth = depths[o][t] + ext * rows[t]
                        depths[o][t] = depth
                        flux = weight * jnp.exp2(depth * slopes[t]) - surface_ref[
                            8 * o : 8 * o + 8, spans[t]
                        ] * jnp.exp2(depth)
                        now[t] = flux if now[t] is None else now[t] + flux
                for t in range(tiles):
                    heats[t].append(jnp.sum(fluxes[t] - now[t], axis=0, keepdims=True))
                    fluxes[t] = now[t]
            for t in range(tiles):
                heat_ref[base, spans[t]] = jnp.concatenate(heats[t], axis=0)
            exts = [pltpu.roll(e, LANES - 8, 1) for e in exts]
            return exts, depths, fluxes

        zero = jnp.zeros((8, LANES), F32)
        lax.fori_loop(
            0,
            LEVELS // 8,
            step,
            (
                [ext_ref[8 * o : 8 * o + 8] for o in range(GROUPS)],
                [[zero] * tiles for _ in range(GROUPS)],
                start,
            ),
        )


def load_extinction(blocks, ext_ref):
    for k in range(4):
        at = 16 * (k & 1)
        ext_ref[14 * k : 14 * k + 14] = blocks[k >> 1][at : at + 14] * SCALE


def octet(count):
    return pl.ds(pl.multiple_of(count * 8, 8), 8)


def spread_row(block, s):
    return jnp.broadcast_to(block[s : s + 1], block.shape)


def sweep(arrays, step, carried, backward=False):
    reads, writes = arrays
    sublane = iota((8, COLS), 0)

    def body(count, carried):
        at = octet(LEVELS // 8 - 1 - count if backward else count)
        blocks = [read(at) for read in reads]
        kept = [None] * len(writes)
        for s in reversed(range(8)) if backward else range(8):
            carried, results = step(carried, *[spread_row(b, s) for b in blocks])
            kept = [r if k is None else jnp.where(sublane == s, r, k) for k, r in zip(kept, results)]
        for write, k in zip(writes, kept):
            write(at, k)
        return carried

    lax.fori_loop(0, LEVELS // 8, body, carried)


def reader(ref, *first):
    return lambda at: ref[(*first, at, slice(None))]


def writer(ref, *first):
    def write(at, value):
        ref[(*first, at, slice(None))] = value

    return write


def factor_kernel(
    scalar_ref, q_ref, wind_ref,
    inv_ref, down_ref, ratio_ref, tend_ref, avg_ref, correct_ref,
    upper_ref, lower_ref, value_ref,
):
    spread = jnp.where(iota((32, COLS), 0) == (iota((32, COLS), 1) >> 4), 1.0, 0.0).astype(BF16)
    row = iota((LANES, COLS), 0)
    weight = jnp.where(row == 32 + (iota((LANES, COLS), 1) >> 4), -2.0, 0.0)
    first = lax.axis_index("elem") * 32
    local = (scalar_ref[ADJACENT:MU, :32].astype(jnp.int32) - first + 32) & 2047
    local = jnp.dot(
        local.astype(F32).astype(BF16), spread, preferred_element_type=F32
    ).astype(jnp.int32)
    for k in range(4):
        weight = weight + jnp.where(row == local[k : k + 1], 0.5, 0.0)
    correct_ref[...] = weight.astype(BF16)
    u, v = wind_ref[0], wind_ref[1]
    mix = scalar_ref[STRENGTH : STRENGTH + 1] * (1.0 + ((u[:-1] - u[1:]) ** 2 + (v[:-1] - v[1:]) ** 2))
    edge = jnp.zeros((1, COLS), F32)
    upper_ref[...] = jnp.concatenate([edge, mix], axis=0)
    lower_ref[...] = jnp.concatenate([mix, edge], axis=0)

    def forward(carried, upper, lower, *sides):
        ratio, values = carried
        inverse = 1.0 / ((1.0 + upper + lower) - upper * ratio)
        ratio = lower * inverse
        down = upper * inverse
        values = [side * inverse + down * value for side, value in zip(sides, values)]
        return (ratio, values), (inverse, down, ratio, *values)

    zero = jnp.zeros((8, COLS), F32)
    sides = [reader(q_ref), reader(wind_ref, 0), reader(wind_ref, 1)]
    sweep(
        (
            [reader(upper_ref), reader(lower_ref), *sides],
            [writer(inv_ref), writer(down_ref), writer(ratio_ref)]
            + [writer(value_ref, f) for f in range(3)],
        ),
        forward,
        (zero, [zero] * 3),
    )

    def backward(solved, ratio, *values):
        solved = [value + ratio * x for value, x in zip(values, solved)]
        return solved, solved

    sweep(
        (
            [reader(ratio_ref)] + [reader(value_ref, f) for f in range(3)],
            [writer(value_ref, f) for f in range(3)],
        ),
        backward,
        [zero] * 3,
        True,
    )
    tend_ref[0] = value_ref[0] - q_ref[...]
    tend_ref[1:3] = value_ref[1:3] - wind_ref[...]
    avg = jnp.zeros((LEVELS, LANES), F32)
    for f in range(3):
        avg = avg + times(tend_ref[f], element_mean(f + 1))
    avg_ref[...] = avg


def home_kernel(
    e0, e1, t_ref, q_ref, scalar_ref, out_ref, a_ref, ext_ref, weight_ref, surface_ref
):
    load_extinction((e0, e1), ext_ref)
    a_ref[...] = t_ref[...] * q_ref[...]
    mu, albedo = scalar_ref[MU : MU + 1], scalar_ref[ALBEDO : ALBEDO + 1]
    heat_columns(a_ref, out_ref, ext_ref, weight_ref, surface_ref, mu, albedo, 4)
    out_ref[...] = out_ref[...] * scalar_ref[LIT : LIT + 1]


def solve_kernel(t_ref, flux_ref, inv_ref, down_ref, ratio_ref, early_ref, tend_ref, avg_ref, heat_ref):
    side = t_ref[...] + flux_ref[...]
    heat_ref[...] = side * inv_ref[...]

    def forward(value, side, down):
        value = side + down * value
        return value, (value,)

    def backward(solved, value, ratio):
        solved = value + ratio * solved
        return solved, (solved,)

    zero = jnp.zeros((8, COLS), F32)
    writes = [writer(heat_ref)]
    sweep(([reader(heat_ref), reader(down_ref)], writes), forward, zero)
    sweep(([reader(heat_ref), reader(ratio_ref)], writes), backward, zero, True)
    tend = heat_ref[...] - t_ref[...]
    tend_ref[...] = tend
    avg_ref[...] = early_ref[...] + times(tend, element_mean(0))


def span_kernel(
    e0, e1, b0, b1, b2, b3, last_ref, out_ref, token_ref,
    a_ref, heat_ref, ext_ref, weight_ref, surface_ref,
):
    load_extinction((e0, e1), ext_ref)
    place = lax.axis_index("elem")
    halves = list(held((b0, b1, b2, b3, last_ref.at[:, :WIDE])))
    for bit in range(3):
        turn = ((place >> bit) & 1) == 1
        height = 1 << bit
        clear = bit_of_row(bit) == 0
        halves = [
            jnp.where(
                turn, jnp.where(clear, pltpu.roll(x, 8 - height, 0), pltpu.roll(x, height, 0)), x
            )
            for x in halves
        ]
    turn = ((place >> 3) & 1) == 1
    low, high = halves
    halves = (jnp.where(turn, high, low), jnp.where(turn, low, high))
    for half in range(2):
        for o in range(10):
            a_ref[8 * o : 8 * o + 8, LANES * half : LANES * half + LANES] = swap_groups(
                halves[half][:, LANES * o : LANES * o + LANES]
            )
    mu = a_ref[LEVELS : LEVELS + 1, :]
    albedo = a_ref[LEVELS + 1 : LEVELS + 2, :]
    occupied = mu > 0.0
    heat_columns(
        a_ref, heat_ref, ext_ref, weight_ref, surface_ref, jnp.where(occupied, mu, 1.0), albedo, 2
    )
    out_ref[...] = jnp.where(occupied, heat_ref[...], 0.0)
    token_ref[...] = jnp.zeros_like(token_ref)


def finish_kernel(tend0_ref, tend_ref, avg_ref, chip_ref, off_ref, correct_ref, out_ref):
    lane = iota((LEVELS, LANES), 1)
    first = (lax.axis_index("elem") & 1) == 0
    own, off = avg_ref[...], off_ref[...]
    chip = jnp.concatenate(
        [chip_ref[:, WIDE + LANES * o : WIDE + LANES * o + LANES] for o in range(LEVELS // 8)], axis=0
    )
    left, right = jnp.where(first, off, chip), jnp.where(first, chip, off)
    table = correct_ref[...]

    def turned(x, by):
        by = by % LANES
        return pltpu.roll(x, by, 1) if by else x

    for f in range(4):
        wide = jnp.where(
            lane < 32,
            turned(left, -32 * f),
            jnp.where(lane < 64, turned(own, 32 - 32 * f), turned(right, 64 - 32 * f)),
        )
        wide = jnp.where(lane < 96, wide, 0.0)
        tend = tend0_ref[...] if f == 0 else tend_ref[f - 1]
        out_ref[f] = tend + times(wide, table)


def call(kernel, outs, scratch, *args, limit=32, after=()):
    idle = len(after)

    def body(*refs):
        kernel(*refs[: len(args)], *refs[len(args) + idle :])

    return pl.pallas_call(
        body,
        out_shape=outs,
        in_specs=[VMEM] * len(args) + [pl.BlockSpec(memory_space=pl.ANY)] * idle,
        out_specs=jax.tree.map(lambda _: VMEM, outs),
        scratch_shapes=scratch,
        compiler_params=pltpu.CompilerParams(vmem_limit_bytes=limit * 1024 * 1024),
    )(*args, *after)


def shape(*dims, dtype=F32):
    return jax.ShapeDtypeStruct(dims, dtype)


def number(s, m):
    return 4 * s + m


BESIDE = [(number(s, m), number(s, m ^ 1)) for s in range(64) for m in range(4)]
OPPOSITE = [(number(s, m), number(s, m ^ 2)) for s in range(64) for m in range(4)]
SWAPS = [
    [(number(s, m), number(s ^ (1 << bit), m)) for s in range(64) for m in range(4)]
    for bit in range(4)
]
ACROSS = [
    [
        (number(16 * g + i, m), number(16 * ((2 * g + 2 - m) % 4) + (i ^ flip), g))
        for g in range(4)
        for i in range(16)
        for m in range(4)
    ]
    for flip in (0, 8)
]
OFF_CHIP = [
    (number(s, m), number((s - 1 if s % 2 == 0 else s + 1) % 64, m))
    for s in range(64)
    for m in range(4)
]


def shards(
    thermal_state,
    moisture_content,
    lateral_velocity_components,
    sun_elevation_factor,
    surface_albedo_values,
    turbulent_diffusion_strength,
    sunlit_indicator,
    destination_partition,
    adjacent_elements,
    optical_extinction,
    insolation_quadrature_share,
):
    row = lambda x: x.reshape(1, COLS)
    mu, albedo = row(sun_elevation_factor), row(surface_albedo_values)
    lit, strength = row(sunlit_indicator), row(turbulent_diffusion_strength)
    field = shape(LEVELS, COLS)
    message = shape(8, WIDE)
    own_ext = jnp.pad(
        jnp.concatenate([optical_extinction, insolation_quadrature_share[:, None]], axis=1),
        ((0, 2), (0, LANES - LEVELS - 1)),
    )
    low, high, scalars = call(
        pack_kernel,
        [message, message, shape(8, COLS)],
        [],
        thermal_state,
        moisture_content,
        mu,
        albedo,
        lit,
        row(destination_partition),
        strength,
        adjacent_elements.T,
        limit=60,
    )
    blocks = [lax.ppermute(x, AXES, pairs) for x, pairs in zip((low, high), ACROSS)]
    beside = lax.ppermute(own_ext, AXES, BESIDE)
    pair = call(pair_kernel, shape(32, LANES), [], own_ext, beside)
    exts = (pair, lax.ppermute(pair, AXES, OPPOSITE))
    inverse, down, ratio, tend_late, early, correct = call(
        factor_kernel,
        [
            field, field, field, shape(3, LEVELS, COLS), shape(LEVELS, LANES),
            shape(LANES, COLS, dtype=BF16),
        ],
        [
            *[pltpu.VMEM((LEVELS, COLS), F32)] * 2,
            pltpu.VMEM((3, LEVELS, COLS), F32),
        ],
        scalars,
        moisture_content,
        lateral_velocity_components,
        after=(pair,),
    )

    def tables(columns):
        return [
            pltpu.VMEM((56, LANES), F32),
            pltpu.VMEM((56, LANES), F32),
            pltpu.VMEM((56, columns), F32),
        ]

    sent = call(next_kernel, message, [], *blocks, after=(early, exts[1]))
    blocks.append(lax.ppermute(sent, AXES, SWAPS[2]))
    heat = call(
        home_kernel,
        field,
        [pltpu.VMEM((LEVELS, COLS), F32), *tables(COLS)],
        *exts, thermal_state, moisture_content, scalars,
        after=(sent,),
    )
    sent = call(next_kernel, message, [], *blocks, after=(heat,))
    blocks.append(lax.ppermute(sent, AXES, SWAPS[1]))
    tend0, average = call(
        solve_kernel,
        [field, shape(LEVELS, LANES)],
        [pltpu.VMEM((LEVELS, COLS), F32)],
        thermal_state, heat, inverse, down, ratio, early,
        after=(sent,),
    )
    off = lax.ppermute(average, AXES, OFF_CHIP)
    sent = call(last_kernel, shape(8, WIDE + LEVELS * 16), [], *blocks, average)
    last = lax.ppermute(sent, AXES, SWAPS[0])
    span_heating, token = call(
        span_kernel,
        [shape(LEVELS, 256), shape(8, LANES)],
        [pltpu.VMEM((80, 256), F32), pltpu.VMEM((LEVELS, 256), F32), *tables(256)],
        *exts, *blocks, last,
    )
    tendency_out = call(
        finish_kernel, shape(4, LEVELS, COLS), [],
        tend0, tend_late, average, last, off, correct,
        after=(token,),
    )
    return tendency_out, span_heating


def solution(mesh):
    return jax.shard_map(
        shards,
        mesh=mesh,
        in_specs=(
            P(None, "elem"),
            P(None, "elem"),
            P(None, None, "elem"),
            P("elem"),
            P("elem"),
            P("elem"),
            P("elem"),
            P("elem", None),
            P("elem", None),
            P("gpt", None),
            P("gpt"),
        ),
        out_specs=(P(None, None, "elem"), P(None, ("elem", "gpt"))),
        check_vma=False,
    )
```

```python
import functools
import math

import jax
import jax.numpy as jnp
from jax import lax
from jax.experimental import pallas as pl
from jax.experimental.pallas import tpu as pltpu
from jax.sharding import PartitionSpec as P

LEVELS = 72
COLS = 512
EPTS = 16
LANES = 128
WIDE = 1280
GROUPS = 7
DIFFUSIVITY = 1.66
SCALE = DIFFUSIVITY * math.log2(math.e)
VMEM = pl.BlockSpec(memory_space=pltpu.VMEM)
AXES = ("elem", "gpt")
BF16 = jnp.bfloat16
F32 = jnp.float32


def iota(shape, dim):
    return lax.broadcasted_iota(jnp.int32, shape, dim)


def split(x):
    high = x.astype(BF16)
    rest = x - high.astype(F32)
    middle = rest.astype(BF16)
    low = (rest - middle.astype(F32)).astype(BF16)
    return jnp.concatenate([high, middle, low], axis=0)


def joined(y):
    rows = y.shape[0] // 3
    return y[:rows] + y[rows : 2 * rows] + y[2 * rows :]


def times(x, table):
    return joined(jnp.dot(split(x), table, preferred_element_type=F32))


def element_mean(field):
    at = field * 32 + (iota((COLS, LANES), 0) >> 4)
    return jnp.where(iota((COLS, LANES), 1) == at, 1.0 / EPTS, 0.0).astype(BF16)


def swap_groups(x):
    sublane, group = iota((8, LANES), 0), iota((8, LANES), 1) >> 4
    for k in range(3):
        height, width = 1 << k, 16 << k
        up = pltpu.roll(pltpu.roll(x, 8 - height, 0), width, 1)
        down = pltpu.roll(pltpu.roll(x, height, 0), LANES - width, 1)
        in_row, in_lane = (sublane >> k) & 1, (group >> k) & 1
        x = jnp.where(in_row == in_lane, x, jnp.where(in_row == 0, up, down))
    return x


STRENGTH, LIT, ADJACENT, MU, ALBEDO = 0, 1, 2, 6, 7


def pack_kernel(
    t_ref, q_ref, mu_ref, albedo_ref, lit_ref, dest_ref, strength_ref, adjacent_ref,
    low_ref, high_ref, scalar_ref,
):
    scalar_ref[STRENGTH : STRENGTH + 1] = strength_ref[...]
    scalar_ref[LIT : LIT + 1] = lit_ref[...].astype(F32)
    scalar_ref[ADJACENT:MU, :32] = adjacent_ref[...].astype(F32)
    scalar_ref[MU : MU + 1] = mu_ref[...]
    scalar_ref[ALBEDO : ALBEDO + 1] = albedo_ref[...]
    served = (2 * (lax.axis_index("elem") >> 4) + 2 - lax.axis_index("gpt")) & 3
    before = jnp.where(iota((LANES, LANES), 0) < iota((LANES, LANES), 1), 1.0, 0.0).astype(BF16)
    dest = dest_ref[...]
    number_of = iota((64, LANES), 0)
    gone = jnp.zeros((64, 1), F32)
    ranks = []
    for tile in range(COLS // LANES):
        onehot = jnp.where(dest[:, LANES * tile : LANES * tile + LANES] == number_of, 1.0, 0.0)
        earlier = jnp.dot(onehot.astype(BF16), before, preferred_element_type=F32)
        ranks.append(jnp.sum(onehot * (earlier + gone), axis=0, keepdims=True))
        gone = gone + jnp.sum(onehot, axis=1, keepdims=True)
    rank = jnp.concatenate(ranks, axis=1).astype(jnp.int32)
    sent = ((dest >> 4) == served) & (lit_ref[...] != 0)
    apart = (dest ^ lax.axis_index("elem") ^ 1) & 15
    slot = jnp.where(sent, coded(apart) * 16 + rank, -1)
    chosen = jnp.where(slot == iota((256, COLS), 0), 1.0, 0.0).astype(BF16)
    row = iota((8, COLS), 0)
    tail = jnp.where(row == 0, mu_ref[...], jnp.where(row == 1, albedo_ref[...], 0.0))
    table = jnp.concatenate([t_ref[...] * q_ref[...], tail], axis=0)
    packed = joined(
        lax.dot_general(
            split(table), chosen, (((1,), (1,)), ((), ())), preferred_element_type=F32
        )
    )
    for half, out_ref in enumerate((low_ref, high_ref)):
        for o in range(10):
            part = packed[8 * o : 8 * o + 8, LANES * half : LANES * half + LANES]
            at = slice(LANES * o, LANES * o + LANES)
            out_ref[:, at] = swap_groups(part)


def coded(apart):
    return apart ^ (((apart >> 1) ^ (apart >> 2)) & 1)


def bit_of_row(bit):
    return (iota((8, WIDE), 0) >> bit) & 1


def taken(low, high, bit):
    return jnp.where(bit_of_row(bit) == 0, pltpu.roll(low, 8 - (1 << bit), 0), high)


def put(low, high, got, bit):
    clear = bit_of_row(bit) == 0
    return jnp.where(clear, low, pltpu.roll(got, 1 << bit, 0)), jnp.where(clear, high, got)


def held(blocks):
    low, high = blocks[0][...], blocks[1][...]
    for bit, got in zip((2, 1, 0), blocks[2:]):
        low, high = put(low, high, got[...], bit)
    return low, high


def next_kernel(*refs):
    *blocks, out_ref = refs
    low, high = held(blocks)
    out_ref[...] = taken(low, high, 4 - len(blocks))


def last_kernel(b0, b1, b2, b3, avg_ref, out_ref):
    low, high = held((b0, b1, b2, b3))
    out_ref[:, :WIDE] = taken(low, high, 0)
    for o in range(LEVELS // 8):
        out_ref[:, WIDE + LANES * o : WIDE + LANES * o + LANES] = avg_ref[8 * o : 8 * o + 8]


def heat_columns(a_ref, heat_ref, ext_ref, weight_ref, surface_ref, mu, albedo, tiles):
    columns = a_ref.shape[1]
    slope = -1.0 / (DIFFUSIVITY * mu)
    total = jnp.dot(
        ext_ref[:, :LEVELS],
        a_ref[:LEVELS, :],
        precision=lax.Precision.HIGHEST,
        preferred_element_type=F32,
    )
    weight_ref[...] = jnp.broadcast_to(ext_ref[:, LEVELS : LEVELS + 1] * (1.0 / SCALE), (56, LANES))
    for tile in range(columns // LANES):
        at = slice(LANES * tile, LANES * tile + LANES)
        surface_ref[:, at] = (
            weight_ref[...] * albedo[:, at] * jnp.exp2(total[:, at] * (slope[:, at] - 1.0))
        )
    for first in range(0, columns // LANES, tiles):
        spans = [slice(LANES * t, LANES * t + LANES) for t in range(first, first + tiles)]
        slopes = [jnp.broadcast_to(slope[:, at], (8, LANES)) for at in spans]
        start = []
        for at in spans:
            flux = jnp.zeros((8, LANES), F32)
            for o in range(GROUPS):
                flux = flux + (weight_ref[8 * o : 8 * o + 8] - surface_ref[8 * o : 8 * o + 8, at])
            start.append(flux)

        def step(octet, carried, spans=spans, slopes=slopes):
            exts, depths, fluxes = carried
            depths, fluxes = [list(d) for d in depths], list(fluxes)
            base = pl.ds(pl.multiple_of(octet * 8, 8), 8)
            arrays = [a_ref[base, at] for at in spans]
            heats = [[] for _ in spans]
            for s in range(8):
                rows = [jnp.broadcast_to(a[s : s + 1], (8, LANES)) for a in arrays]
                now = [None] * tiles
                for o in range(GROUPS):
                    ext = jnp.broadcast_to(exts[o][:, s : s + 1], (8, LANES))
                    weight = weight_ref[8 * o : 8 * o + 8]
                    for t in range(tiles):
                        depth = depths[o][t] + ext * rows[t]
                        depths[o][t] = depth
                        flux = weight * jnp.exp2(depth * slopes[t]) - surface_ref[
                            8 * o : 8 * o + 8, spans[t]
                        ] * jnp.exp2(depth)
                        now[t] = flux if now[t] is None else now[t] + flux
                for t in range(tiles):
                    heats[t].append(jnp.sum(fluxes[t] - now[t], axis=0, keepdims=True))
                    fluxes[t] = now[t]
            for t in range(tiles):
                heat_ref[base, spans[t]] = jnp.concatenate(heats[t], axis=0)
            exts = [pltpu.roll(e, LANES - 8, 1) for e in exts]
            return exts, depths, fluxes

        zero = jnp.zeros((8, LANES), F32)
        lax.fori_loop(
            0,
            LEVELS // 8,
            step,
            (
                [ext_ref[8 * o : 8 * o + 8] for o in range(GROUPS)],
                [[zero] * tiles for _ in range(GROUPS)],
                start,
            ),
        )


def load_extinction(blocks, ext_ref):
    for k, block in enumerate(blocks):
        ext_ref[14 * k : 14 * k + 14] = block[:14] * SCALE


def octet(count):
    return pl.ds(pl.multiple_of(count * 8, 8), 8)


def spread_row(block, s):
    return jnp.broadcast_to(block[s : s + 1], block.shape)


def sweep(arrays, step, carried, backward=False):
    reads, writes = arrays
    sublane = iota((8, COLS), 0)

    def body(count, carried):
        at = octet(LEVELS // 8 - 1 - count if backward else count)
        blocks = [read(at) for read in reads]
        kept = [None] * len(writes)
        for s in reversed(range(8)) if backward else range(8):
            carried, results = step(carried, *[spread_row(b, s) for b in blocks])
            kept = [r if k is None else jnp.where(sublane == s, r, k) for k, r in zip(kept, results)]
        for write, k in zip(writes, kept):
            write(at, k)
        return carried

    lax.fori_loop(0, LEVELS // 8, body, carried)


def reader(ref, *first):
    return lambda at: ref[(*first, at, slice(None))]


def writer(ref, *first):
    def write(at, value):
        ref[(*first, at, slice(None))] = value

    return write


def factor_kernel(
    scalar_ref, q_ref, wind_ref,
    inv_ref, down_ref, ratio_ref, tend_ref,
    upper_ref, lower_ref, value_ref,
):
    u, v = wind_ref[0], wind_ref[1]
    mix = scalar_ref[STRENGTH : STRENGTH + 1] * (1.0 + ((u[:-1] - u[1:]) ** 2 + (v[:-1] - v[1:]) ** 2))
    edge = jnp.zeros((1, COLS), F32)
    upper_ref[...] = jnp.concatenate([edge, mix], axis=0)
    lower_ref[...] = jnp.concatenate([mix, edge], axis=0)

    def forward(carried, upper, lower, *sides):
        ratio, values = carried
        inverse = 1.0 / ((1.0 + upper + lower) - upper * ratio)
        ratio = lower * inverse
        down = upper * inverse
        values = [side * inverse + down * value for side, value in zip(sides, values)]
        return (ratio, values), (inverse, down, ratio, *values)

    zero = jnp.zeros((8, COLS), F32)
    sides = [reader(q_ref), reader(wind_ref, 0), reader(wind_ref, 1)]
    sweep(
        (
            [reader(upper_ref), reader(lower_ref), *sides],
            [writer(inv_ref), writer(down_ref), writer(ratio_ref)]
            + [writer(value_ref, f) for f in range(3)],
        ),
        forward,
        (zero, [zero] * 3),
    )

    def backward(solved, ratio, *values):
        solved = [value + ratio * x for value, x in zip(values, solved)]
        return solved, solved

    sweep(
        (
            [reader(ratio_ref)] + [reader(value_ref, f) for f in range(3)],
            [writer(value_ref, f) for f in range(3)],
        ),
        backward,
        [zero] * 3,
        True,
    )
    tend_ref[0] = value_ref[0] - q_ref[...]
    tend_ref[1:3] = value_ref[1:3] - wind_ref[...]


def home_kernel(
    e0, e1, e2, e3, t_ref, q_ref, scalar_ref, out_ref, a_ref, ext_ref, weight_ref, surface_ref
):
    load_extinction((e0, e1, e2, e3), ext_ref)
    a_ref[...] = t_ref[...] * q_ref[...]
    mu, albedo = scalar_ref[MU : MU + 1], scalar_ref[ALBEDO : ALBEDO + 1]
    heat_columns(a_ref, out_ref, ext_ref, weight_ref, surface_ref, mu, albedo, 4)
    out_ref[...] = out_ref[...] * scalar_ref[LIT : LIT + 1]


def solve_kernel(
    t_ref, flux_ref, inv_ref, down_ref, ratio_ref, late_ref, scalar_ref,
    tend_ref, avg_ref, correct_ref,
    heat_ref,
):
    side = t_ref[...] + flux_ref[...]
    heat_ref[...] = side * inv_ref[...]

    def forward(value, side, down):
        value = side + down * value
        return value, (value,)

    def backward(solved, value, ratio):
        solved = value + ratio * solved
        return solved, (solved,)

    zero = jnp.zeros((8, COLS), F32)
    writes = [writer(heat_ref)]
    sweep(([reader(heat_ref), reader(down_ref)], writes), forward, zero)
    sweep(([reader(heat_ref), reader(ratio_ref)], writes), backward, zero, True)
    tend = heat_ref[...] - t_ref[...]
    tend_ref[...] = tend
    avg = times(tend, element_mean(0))
    for f in range(3):
        avg = avg + times(late_ref[f], element_mean(f + 1))
    avg_ref[...] = avg
    spread = jnp.where(iota((32, COLS), 0) == (iota((32, COLS), 1) >> 4), 1.0, 0.0).astype(BF16)
    row = iota((LANES, COLS), 0)
    weight = jnp.where(row == 32 + (iota((LANES, COLS), 1) >> 4), -2.0, 0.0)
    first = lax.axis_index("elem") * 32
    local = (scalar_ref[ADJACENT:MU, :32].astype(jnp.int32) - first + 32) & 2047
    local = jnp.dot(
        local.astype(F32).astype(BF16), spread, preferred_element_type=F32
    ).astype(jnp.int32)
    for k in range(4):
        weight = weight + jnp.where(row == local[k : k + 1], 0.5, 0.0)
    correct_ref[...] = weight.astype(BF16)


def span_kernel(
    e0, e1, e2, e3, b0, b1, b2, b3, last_ref, out_ref, token_ref,
    a_ref, heat_ref, ext_ref, weight_ref, surface_ref,
):
    load_extinction((e0, e1, e2, e3), ext_ref)
    place = lax.axis_index("elem") ^ 1
    halves = list(held((b0, b1, b2, b3, last_ref.at[:, :WIDE])))
    mixed = (bit_of_row(1) ^ bit_of_row(2)) & 1
    for bit in range(3):
        turn = ((place >> bit) & 1) == 1
        if bit == 0:
            turn = ((place & 1) ^ mixed) == 1
        height = 1 << bit
        clear = bit_of_row(bit) == 0
        halves = [
            jnp.where(
                turn, jnp.where(clear, pltpu.roll(x, 8 - height, 0), pltpu.roll(x, height, 0)), x
            )
            for x in halves
        ]
    turn = ((place >> 3) & 1) == 1
    low, high = halves
    halves = (jnp.where(turn, high, low), jnp.where(turn, low, high))
    for half in range(2):
        for o in range(10):
            a_ref[8 * o : 8 * o + 8, LANES * half : LANES * half + LANES] = swap_groups(
                halves[half][:, LANES * o : LANES * o + LANES]
            )
    mu = a_ref[LEVELS : LEVELS + 1, :]
    albedo = a_ref[LEVELS + 1 : LEVELS + 2, :]
    occupied = mu > 0.0
    heat_columns(
        a_ref, heat_ref, ext_ref, weight_ref, surface_ref, jnp.where(occupied, mu, 1.0), albedo, 2
    )
    out_ref[...] = jnp.where(occupied, heat_ref[...], 0.0)
    token_ref[...] = jnp.zeros_like(token_ref)


def finish_kernel(tend0_ref, tend_ref, avg_ref, chip_ref, off_ref, correct_ref, out_ref):
    lane = iota((LEVELS, LANES), 1)
    first = (lax.axis_index("elem") & 1) == 0
    own, off = avg_ref[...], off_ref[...]
    chip = jnp.concatenate(
        [chip_ref[:, WIDE + LANES * o : WIDE + LANES * o + LANES] for o in range(LEVELS // 8)], axis=0
    )
    left, right = jnp.where(first, off, chip), jnp.where(first, chip, off)
    table = correct_ref[...]

    def turned(x, by):
        by = by % LANES
        return pltpu.roll(x, by, 1) if by else x

    for f in range(4):
        wide = jnp.where(
            lane < 32,
            turned(left, -32 * f),
            jnp.where(lane < 64, turned(own, 32 - 32 * f), turned(right, 64 - 32 * f)),
        )
        wide = jnp.where(lane < 96, wide, 0.0)
        tend = tend0_ref[...] if f == 0 else tend_ref[f - 1]
        out_ref[f] = tend + times(wide, table)


def call(kernel, outs, scratch, *args, limit=32, after=()):
    idle = len(after)

    def body(*refs):
        kernel(*refs[: len(args)], *refs[len(args) + idle :])

    return pl.pallas_call(
        body,
        out_shape=outs,
        in_specs=[VMEM] * len(args) + [pl.BlockSpec(memory_space=pl.ANY)] * idle,
        out_specs=jax.tree.map(lambda _: VMEM, outs),
        scratch_shapes=scratch,
        compiler_params=pltpu.CompilerParams(vmem_limit_bytes=limit * 1024 * 1024),
    )(*args, *after)


def shape(*dims, dtype=F32):
    return jax.ShapeDtypeStruct(dims, dtype)


def number(s, m):
    return 4 * s + m


ASIDE = [
    [(number(s, m), number(s ^ 1, m ^ move)) for s in range(64) for m in range(4)]
    for move in (1, 2, 3)
]
SWAPS = [
    [(number(s, m), number(s ^ move, m)) for s in range(64) for m in range(4)]
    for move in (1, 3, 5)
]
ACROSS = [
    [
        (number(16 * g + i, m), number(16 * ((2 * g + 2 - m) % 4) + (i ^ flip), g))
        for g in range(4)
        for i in range(16)
        for m in range(4)
    ]
    for flip in (1, 9)
]
OFF_CHIP = [
    (number(s, m), number((s - 1 if s % 2 == 0 else s + 1) % 64, m))
    for s in range(64)
    for m in range(4)
]


def shards(
    thermal_state,
    moisture_content,
    lateral_velocity_components,
    sun_elevation_factor,
    surface_albedo_values,
    turbulent_diffusion_strength,
    sunlit_indicator,
    destination_partition,
    adjacent_elements,
    optical_extinction,
    insolation_quadrature_share,
):
    row = lambda x: x.reshape(1, COLS)
    mu, albedo = row(sun_elevation_factor), row(surface_albedo_values)
    lit, strength = row(sunlit_indicator), row(turbulent_diffusion_strength)
    field = shape(LEVELS, COLS)
    message = shape(8, WIDE)
    own_ext = jnp.pad(
        jnp.concatenate([optical_extinction, insolation_quadrature_share[:, None]], axis=1),
        ((0, 2), (0, LANES - LEVELS - 1)),
    )
    low, high, scalars = call(
        pack_kernel,
        [message, message, shape(8, COLS)],
        [],
        thermal_state,
        moisture_content,
        mu,
        albedo,
        lit,
        row(destination_partition),
        strength,
        adjacent_elements.T,
        limit=60,
    )
    blocks = [lax.ppermute(x, AXES, pairs) for x, pairs in zip((low, high), ACROSS)]
    exts = [own_ext] + [lax.ppermute(own_ext, AXES, pairs) for pairs in ASIDE]
    inverse, down, ratio, tend_late = call(
        factor_kernel,
        [
            field, field, field, shape(3, LEVELS, COLS),
        ],
        [
            *[pltpu.VMEM((LEVELS, COLS), F32)] * 2,
            pltpu.VMEM((3, LEVELS, COLS), F32),
        ],
        scalars,
        moisture_content,
        lateral_velocity_components,
    )

    def tables(columns):
        return [
            pltpu.VMEM((56, LANES), F32),
            pltpu.VMEM((56, LANES), F32),
            pltpu.VMEM((56, columns), F32),
        ]

    sent = call(next_kernel, message, [], *blocks, after=(ratio, *exts[1:]))
    blocks.append(lax.ppermute(sent, AXES, SWAPS[2]))
    heat = call(
        home_kernel,
        field,
        [pltpu.VMEM((LEVELS, COLS), F32), *tables(COLS)],
        *exts, thermal_state, moisture_content, scalars,
        after=(sent,),
    )
    sent = call(next_kernel, message, [], *blocks, after=(heat,))
    blocks.append(lax.ppermute(sent, AXES, SWAPS[1]))
    tend0, average, correct = call(
        solve_kernel,
        [field, shape(LEVELS, LANES), shape(LANES, COLS, dtype=BF16)],
        [pltpu.VMEM((LEVELS, COLS), F32)],
        thermal_state, heat, inverse, down, ratio, tend_late, scalars,
        after=(sent,),
    )
    off = lax.ppermute(average, AXES, OFF_CHIP)
    sent = call(last_kernel, shape(8, WIDE + LEVELS * 16), [], *blocks, average)
    last = lax.ppermute(sent, AXES, SWAPS[0])
    span_heating, token = call(
        span_kernel,
        [shape(LEVELS, 256), shape(8, LANES)],
        [pltpu.VMEM((80, 256), F32), pltpu.VMEM((LEVELS, 256), F32), *tables(256)],
        *exts, *blocks, last,
    )
    tendency_out = call(
        finish_kernel, shape(4, LEVELS, COLS), [],
        tend0, tend_late, average, last, off, correct,
        after=(token,),
    )
    return tendency_out, span_heating


def solution(mesh):
    return jax.shard_map(
        shards,
        mesh=mesh,
        in_specs=(
            P(None, "elem"),
            P(None, "elem"),
            P(None, None, "elem"),
            P("elem"),
            P("elem"),
            P("elem"),
            P("elem"),
            P("elem", None),
            P("elem", None),
            P("gpt", None),
            P("gpt"),
        ),
        out_specs=(P(None, None, "elem"), P(None, ("elem", "gpt"))),
        check_vma=False,
    )
```

```python
import functools
import math

import jax
import jax.numpy as jnp
from jax import lax
from jax.experimental import pallas as pl
from jax.experimental.pallas import tpu as pltpu
from jax.sharding import PartitionSpec as P

LEVELS = 72
COLS = 512
EPTS = 16
LANES = 128
WIDE = 1280
GROUPS = 7
DIFFUSIVITY = 1.66
SCALE = DIFFUSIVITY * math.log2(math.e)
VMEM = pl.BlockSpec(memory_space=pltpu.VMEM)
ANY = pl.BlockSpec(memory_space=pl.ANY)
AXES = ("elem", "gpt")
BF16 = jnp.bfloat16
F32 = jnp.float32


def iota(shape, dim):
    return lax.broadcasted_iota(jnp.int32, shape, dim)


def split(x):
    high = x.astype(BF16)
    rest = x - high.astype(F32)
    middle = rest.astype(BF16)
    low = (rest - middle.astype(F32)).astype(BF16)
    return jnp.concatenate([high, middle, low], axis=0)


def joined(y):
    rows = y.shape[0] // 3
    return y[:rows] + y[rows : 2 * rows] + y[2 * rows :]


def times(x, table):
    return joined(jnp.dot(split(x), table, preferred_element_type=F32))


def element_mean(field):
    at = field * 32 + (iota((COLS, LANES), 0) >> 4)
    return jnp.where(iota((COLS, LANES), 1) == at, 1.0 / EPTS, 0.0).astype(BF16)


def swap_groups(x):
    sublane, group = iota((8, LANES), 0), iota((8, LANES), 1) >> 4
    for k in range(3):
        height, width = 1 << k, 16 << k
        up = pltpu.roll(pltpu.roll(x, 8 - height, 0), width, 1)
        down = pltpu.roll(pltpu.roll(x, height, 0), LANES - width, 1)
        in_row, in_lane = (sublane >> k) & 1, (group >> k) & 1
        x = jnp.where(in_row == in_lane, x, jnp.where(in_row == 0, up, down))
    return x


STRENGTH, LIT, ADJACENT, MU, ALBEDO = 0, 1, 2, 6, 7


def pack_kernel(*refs):
    sources, (low_ref, high_ref, scalar_ref), targets, sems = refs[:8], refs[8:11], refs[11:19], refs[19]
    copies = [
        pltpu.make_async_copy(source, target, sems.at[k])
        for k, (source, target) in enumerate(zip(sources, targets))
    ]
    for copy in copies:
        copy.start()
    dest_ref, lit_ref, t_ref, q_ref, mu_ref, albedo_ref, strength_ref, adjacent_ref = targets
    served = (2 * (lax.axis_index("elem") >> 4) + 2 - lax.axis_index("gpt")) & 3
    before = jnp.where(iota((LANES, LANES), 0) < iota((LANES, LANES), 1), 1.0, 0.0).astype(BF16)
    copies[0].wait()
    copies[1].wait()
    dest = dest_ref[...]
    number_of = iota((64, LANES), 0)
    gone = jnp.zeros((64, 1), F32)
    ranks = []
    for tile in range(COLS // LANES):
        onehot = jnp.where(dest[:, LANES * tile : LANES * tile + LANES] == number_of, 1.0, 0.0)
        earlier = jnp.dot(onehot.astype(BF16), before, preferred_element_type=F32)
        ranks.append(jnp.sum(onehot * (earlier + gone), axis=0, keepdims=True))
        gone = gone + jnp.sum(onehot, axis=1, keepdims=True)
    rank = jnp.concatenate(ranks, axis=1).astype(jnp.int32)
    sent = ((dest >> 4) == served) & (lit_ref[...] != 0)
    apart = (dest ^ lax.axis_index("elem") ^ 1) & 15
    slot = jnp.where(sent, coded(apart) * 16 + rank, -1)
    chosen = jnp.where(slot == iota((256, COLS), 0), 1.0, 0.0).astype(BF16)
    for copy in copies[2:]:
        copy.wait()
    scalar_ref[STRENGTH : STRENGTH + 1] = strength_ref[...]
    scalar_ref[LIT : LIT + 1] = lit_ref[...].astype(F32)
    scalar_ref[ADJACENT:MU, :32] = adjacent_ref[...].astype(F32)
    scalar_ref[MU : MU + 1] = mu_ref[...]
    scalar_ref[ALBEDO : ALBEDO + 1] = albedo_ref[...]
    row = iota((8, COLS), 0)
    tail = jnp.where(row == 0, mu_ref[...], jnp.where(row == 1, albedo_ref[...], 0.0))
    table = jnp.concatenate([t_ref[...] * q_ref[...], tail], axis=0)
    packed = joined(
        lax.dot_general(
            split(table), chosen, (((1,), (1,)), ((), ())), preferred_element_type=F32
        )
    )
    for half, out_ref in enumerate((low_ref, high_ref)):
        for o in range(10):
            part = packed[8 * o : 8 * o + 8, LANES * half : LANES * half + LANES]
            at = slice(LANES * o, LANES * o + LANES)
            out_ref[:, at] = swap_groups(part)


def coded(apart):
    return apart ^ (((apart >> 1) ^ (apart >> 2)) & 1)


def bit_of_row(bit):
    return (iota((8, WIDE), 0) >> bit) & 1


def taken(low, high, bit):
    return jnp.where(bit_of_row(bit) == 0, pltpu.roll(low, 8 - (1 << bit), 0), high)


def put(low, high, got, bit):
    clear = bit_of_row(bit) == 0
    return jnp.where(clear, low, pltpu.roll(got, 1 << bit, 0)), jnp.where(clear, high, got)


def held(blocks):
    low, high = blocks[0][...], blocks[1][...]
    for bit, got in zip((2, 1, 0), blocks[2:]):
        low, high = put(low, high, got[...], bit)
    return low, high


def next_kernel(*refs):
    *blocks, out_ref = refs
    low, high = held(blocks)
    out_ref[...] = taken(low, high, 4 - len(blocks))


def last_kernel(b0, b1, b2, b3, avg_ref, out_ref):
    low, high = held((b0, b1, b2, b3))
    out_ref[:, :WIDE] = taken(low, high, 0)
    for o in range(LEVELS // 8):
        out_ref[:, WIDE + LANES * o : WIDE + LANES * o + LANES] = avg_ref[8 * o : 8 * o + 8]


def heat_columns(a_ref, heat_ref, ext_ref, weight_ref, surface_ref, parts_ref, mu, albedo, tiles):
    columns = a_ref.shape[1]
    slope = -1.0 / (DIFFUSIVITY * mu)
    total = jnp.dot(
        ext_ref[:, :LEVELS],
        a_ref[:LEVELS, :],
        precision=lax.Precision.HIGHEST,
        preferred_element_type=F32,
    )
    weight_ref[...] = jnp.broadcast_to(ext_ref[:, LEVELS : LEVELS + 1] * (1.0 / SCALE), (56, LANES))
    for tile in range(columns // LANES):
        at = slice(LANES * tile, LANES * tile + LANES)
        surface_ref[:, at] = (
            weight_ref[...] * albedo[:, at] * jnp.exp2(total[:, at] * (slope[:, at] - 1.0))
        )
    for first in range(0, columns // LANES, tiles):
        spans = [slice(LANES * t, LANES * t + LANES) for t in range(first, first + tiles)]
        slopes = [jnp.broadcast_to(slope[:, at], (8, LANES)) for at in spans]
        start = []
        for at in spans:
            flux = jnp.zeros((8, LANES), F32)
            for o in range(GROUPS):
                flux = flux + (weight_ref[8 * o : 8 * o + 8] - surface_ref[8 * o : 8 * o + 8, at])
            start.append(flux)

        def step(octet, carried, spans=spans, slopes=slopes, first=first):
            exts, depths, fluxes = carried
            depths, fluxes = [list(d) for d in depths], list(fluxes)
            base = pl.ds(pl.multiple_of(octet * 8, 8), 8)
            arrays = [a_ref[base, at] for at in spans]
            for s in range(8):
                rows = [jnp.broadcast_to(a[s : s + 1], (8, LANES)) for a in arrays]
                now = [None] * tiles
                for o in range(GROUPS):
                    ext = jnp.broadcast_to(exts[o][:, s : s + 1], (8, LANES))
                    weight = weight_ref[8 * o : 8 * o + 8]
                    for t in range(tiles):
                        depth = depths[o][t] + ext * rows[t]
                        depths[o][t] = depth
                        flux = weight * jnp.exp2(depth * slopes[t]) - surface_ref[
                            8 * o : 8 * o + 8, spans[t]
                        ] * jnp.exp2(depth)
                        now[t] = flux if now[t] is None else now[t] + flux
                for t in range(tiles):
                    at = pl.ds(pl.multiple_of(octet * 64 + 8 * s, 8), 8)
                    parts_ref[first + t, at] = fluxes[t] - now[t]
                    fluxes[t] = now[t]
            exts = [pltpu.roll(e, LANES - 8, 1) for e in exts]
            return exts, depths, fluxes

        zero = jnp.zeros((8, LANES), F32)
        lax.fori_loop(
            0,
            LEVELS // 8,
            step,
            (
                [ext_ref[8 * o : 8 * o + 8] for o in range(GROUPS)],
                [[zero] * tiles for _ in range(GROUPS)],
                start,
            ),
            unroll=3,
        )
    for tile in range(columns // LANES):
        heat = parts_ref[tile, pl.ds(0, LEVELS, stride=8), :]
        for s in range(1, 8):
            heat = heat + parts_ref[tile, pl.ds(s, LEVELS, stride=8), :]
        heat_ref[:, LANES * tile : LANES * tile + LANES] = heat


def load_extinction(blocks, ext_ref):
    for k, block in enumerate(blocks):
        ext_ref[14 * k : 14 * k + 14] = block[:14] * SCALE


def octet(count):
    return pl.ds(pl.multiple_of(count * 8, 8), 8)


def spread_row(block, s):
    return jnp.broadcast_to(block[s : s + 1], block.shape)


def sweep(arrays, step, carried, backward=False):
    reads, writes = arrays
    sublane = iota((8, COLS), 0)

    def body(count, carried):
        at = octet(LEVELS // 8 - 1 - count if backward else count)
        blocks = [read(at) for read in reads]
        kept = [None] * len(writes)
        for s in reversed(range(8)) if backward else range(8):
            carried, results = step(carried, *[spread_row(b, s) for b in blocks])
            kept = [r if k is None else jnp.where(sublane == s, r, k) for k, r in zip(kept, results)]
        for write, k in zip(writes, kept):
            write(at, k)
        return carried

    lax.fori_loop(0, LEVELS // 8, body, carried, unroll=3)


def reader(ref, *first):
    return lambda at: ref[(*first, at, slice(None))]


def writer(ref, *first):
    def write(at, value):
        ref[(*first, at, slice(None))] = value

    return write


def factor_kernel(
    scalar_ref, wind_ref,
    inv_ref, down_ref, ratio_ref, tend_ref,
    upper_ref, lower_ref, value_ref,
):
    u, v = wind_ref[0], wind_ref[1]
    mix = scalar_ref[STRENGTH : STRENGTH + 1] * (1.0 + ((u[:-1] - u[1:]) ** 2 + (v[:-1] - v[1:]) ** 2))
    edge = jnp.zeros((1, COLS), F32)
    upper_ref[...] = jnp.concatenate([edge, mix], axis=0)
    lower_ref[...] = jnp.concatenate([mix, edge], axis=0)

    def forward(carried, upper, lower, *sides):
        ratio, values = carried
        inverse = 1.0 / ((1.0 + upper + lower) - upper * ratio)
        ratio = lower * inverse
        down = upper * inverse
        values = [side * inverse + down * value for side, value in zip(sides, values)]
        return (ratio, values), (inverse, down, ratio, *values)

    zero = jnp.zeros((8, COLS), F32)
    sides = [reader(wind_ref, 0), reader(wind_ref, 1)]
    sweep(
        (
            [reader(upper_ref), reader(lower_ref), *sides],
            [writer(inv_ref), writer(down_ref), writer(ratio_ref)]
            + [writer(value_ref, f) for f in range(2)],
        ),
        forward,
        (zero, [zero] * 2),
    )

    def backward(solved, ratio, *values):
        solved = [value + ratio * x for value, x in zip(values, solved)]
        return solved, solved

    sweep(
        (
            [reader(ratio_ref)] + [reader(value_ref, f) for f in range(2)],
            [writer(value_ref, f) for f in range(2)],
        ),
        backward,
        [zero] * 2,
        True,
    )
    tend_ref[...] = value_ref[...] - wind_ref[...]


def home_kernel(
    e0, e1, e2, e3, t_ref, q_ref, scalar_ref, out_ref, a_ref, ext_ref, weight_ref, surface_ref, parts_ref
):
    load_extinction((e0, e1, e2, e3), ext_ref)
    a_ref[...] = t_ref[...] * q_ref[...]
    mu, albedo = scalar_ref[MU : MU + 1], scalar_ref[ALBEDO : ALBEDO + 1]
    heat_columns(a_ref, out_ref, ext_ref, weight_ref, surface_ref, parts_ref, mu, albedo, 4)
    out_ref[...] = out_ref[...] * scalar_ref[LIT : LIT + 1]


def solve_kernel(
    t_ref, q_ref, flux_ref, inv_ref, down_ref, ratio_ref, late_ref, scalar_ref,
    tend_ref, avg_ref, correct_ref,
    side_ref,
):
    side_ref[0] = (t_ref[...] + flux_ref[...]) * inv_ref[...]
    side_ref[1] = q_ref[...] * inv_ref[...]

    def forward(values, down, *sides):
        values = [side + down * value for side, value in zip(sides, values)]
        return values, values

    def backward(solved, ratio, *values):
        solved = [value + ratio * x for value, x in zip(values, solved)]
        return solved, solved

    zero = jnp.zeros((8, COLS), F32)
    sides = [reader(side_ref, f) for f in range(2)]
    writes = [writer(side_ref, f) for f in range(2)]
    sweep(([reader(down_ref), *sides], writes), forward, [zero] * 2)
    sweep(([reader(ratio_ref), *sides], writes), backward, [zero] * 2, True)
    tend_ref[0] = side_ref[0] - t_ref[...]
    tend_ref[1] = side_ref[1] - q_ref[...]
    avg = jnp.zeros((LEVELS, LANES), F32)
    for f in range(2):
        avg = avg + times(tend_ref[f], element_mean(f))
        avg = avg + times(late_ref[f], element_mean(f + 2))
    avg_ref[...] = avg
    spread = jnp.where(iota((32, COLS), 0) == (iota((32, COLS), 1) >> 4), 1.0, 0.0).astype(BF16)
    row = iota((LANES, COLS), 0)
    weight = jnp.where(row == 32 + (iota((LANES, COLS), 1) >> 4), -2.0, 0.0)
    first = lax.axis_index("elem") * 32
    local = (scalar_ref[ADJACENT:MU, :32].astype(jnp.int32) - first + 32) & 2047
    local = jnp.dot(
        local.astype(F32).astype(BF16), spread, preferred_element_type=F32
    ).astype(jnp.int32)
    for k in range(4):
        weight = weight + jnp.where(row == local[k : k + 1], 0.5, 0.0)
    correct_ref[...] = weight.astype(BF16)


def span_kernel(
    e0, e1, e2, e3, b0, b1, b2, b3, last_ref, out_ref, token_ref,
    a_ref, heat_ref, ext_ref, weight_ref, surface_ref, parts_ref,
):
    load_extinction((e0, e1, e2, e3), ext_ref)
    place = lax.axis_index("elem") ^ 1
    halves = list(held((b0, b1, b2, b3, last_ref.at[:, :WIDE])))
    mixed = (bit_of_row(1) ^ bit_of_row(2)) & 1
    for bit in range(3):
        turn = ((place >> bit) & 1) == 1
        if bit == 0:
            turn = ((place & 1) ^ mixed) == 1
        height = 1 << bit
        clear = bit_of_row(bit) == 0
        halves = [
            jnp.where(
                turn, jnp.where(clear, pltpu.roll(x, 8 - height, 0), pltpu.roll(x, height, 0)), x
            )
            for x in halves
        ]
    turn = ((place >> 3) & 1) == 1
    low, high = halves
    halves = (jnp.where(turn, high, low), jnp.where(turn, low, high))
    for half in range(2):
        for o in range(10):
            a_ref[8 * o : 8 * o + 8, LANES * half : LANES * half + LANES] = swap_groups(
                halves[half][:, LANES * o : LANES * o + LANES]
            )
    mu = a_ref[LEVELS : LEVELS + 1, :]
    albedo = a_ref[LEVELS + 1 : LEVELS + 2, :]
    occupied = mu > 0.0
    heat_columns(
        a_ref, heat_ref, ext_ref, weight_ref, surface_ref, parts_ref,
        jnp.where(occupied, mu, 1.0), albedo, 2,
    )
    out_ref[...] = jnp.where(occupied, heat_ref[...], 0.0)
    token_ref[...] = jnp.zeros_like(token_ref)


def finish_kernel(tend0_ref, tend_ref, avg_ref, chip_ref, off_ref, correct_ref, out_hbm, out_ref, sems):
    lane = iota((LEVELS, LANES), 1)
    first = (lax.axis_index("elem") & 1) == 0
    own, off = avg_ref[...], off_ref[...]
    chip = jnp.concatenate(
        [chip_ref[:, WIDE + LANES * o : WIDE + LANES * o + LANES] for o in range(LEVELS // 8)], axis=0
    )
    left, right = jnp.where(first, off, chip), jnp.where(first, chip, off)
    table = correct_ref[...]
    copies = []

    def turned(x, by):
        by = by % LANES
        return pltpu.roll(x, by, 1) if by else x

    for f in range(4):
        wide = jnp.where(
            lane < 32,
            turned(left, -32 * f),
            jnp.where(lane < 64, turned(own, 32 - 32 * f), turned(right, 64 - 32 * f)),
        )
        wide = jnp.where(lane < 96, wide, 0.0)
        tend = (tend0_ref if f < 2 else tend_ref)[f & 1]
        out_ref[f] = tend + times(wide, table)
        copies.append(pltpu.make_async_copy(out_ref.at[f], out_hbm.at[f], sems.at[f]))
        copies[f].start()
    for copy in copies:
        copy.wait()


def call(kernel, outs, scratch, *args, limit=32, after=(), hbm_in=False, hbm_out=False):
    idle = len(after)

    def body(*refs):
        kernel(*refs[: len(args)], *refs[len(args) + idle :])

    return pl.pallas_call(
        body,
        out_shape=outs,
        in_specs=[ANY if hbm_in else VMEM] * len(args) + [ANY] * idle,
        out_specs=jax.tree.map(lambda _: ANY if hbm_out else VMEM, outs),
        scratch_shapes=scratch,
        compiler_params=pltpu.CompilerParams(vmem_limit_bytes=limit * 1024 * 1024),
    )(*args, *after)


def shape(*dims, dtype=F32):
    return jax.ShapeDtypeStruct(dims, dtype)


def number(s, m):
    return 4 * s + m


ASIDE = [
    [(number(s, m), number(s ^ 1, m ^ move)) for s in range(64) for m in range(4)]
    for move in (1, 2, 3)
]
SWAPS = [
    [(number(s, m), number(s ^ move, m)) for s in range(64) for m in range(4)]
    for move in (1, 3, 5)
]
ACROSS = [
    [
        (number(16 * g + i, m), number(16 * ((2 * g + 2 - m) % 4) + (i ^ flip), g))
        for g in range(4)
        for i in range(16)
        for m in range(4)
    ]
    for flip in (1, 9)
]
OFF_CHIP = [
    (number(s, m), number((s - 1 if s % 2 == 0 else s + 1) % 64, m))
    for s in range(64)
    for m in range(4)
]


def shards(
    thermal_state,
    moisture_content,
    lateral_velocity_components,
    sun_elevation_factor,
    surface_albedo_values,
    turbulent_diffusion_strength,
    sunlit_indicator,
    destination_partition,
    adjacent_elements,
    optical_extinction,
    insolation_quadrature_share,
):
    row = lambda x: x.reshape(1, COLS)
    mu, albedo = row(sun_elevation_factor), row(surface_albedo_values)
    lit, strength = row(sunlit_indicator), row(turbulent_diffusion_strength)
    field = shape(LEVELS, COLS)
    message = shape(8, WIDE)
    own_ext = jnp.pad(
        jnp.concatenate([optical_extinction, insolation_quadrature_share[:, None]], axis=1),
        ((0, 2), (0, LANES - LEVELS - 1)),
    )
    params = (
        row(destination_partition), lit, thermal_state, moisture_content,
        mu, albedo, strength, adjacent_elements.T,
    )
    low, high, scalars = call(
        pack_kernel,
        [message, message, shape(8, COLS)],
        [pltpu.VMEM(x.shape, x.dtype) for x in params] + [pltpu.SemaphoreType.DMA((len(params),))],
        *params,
        limit=60,
        hbm_in=True,
    )
    blocks = [lax.ppermute(x, AXES, pairs) for x, pairs in zip((low, high), ACROSS)]
    exts = [own_ext] + [lax.ppermute(own_ext, AXES, pairs) for pairs in ASIDE]
    inverse, down, ratio, tend_late = call(
        factor_kernel,
        [
            field, field, field, shape(2, LEVELS, COLS),
        ],
        [
            *[pltpu.VMEM((LEVELS, COLS), F32)] * 2,
            pltpu.VMEM((2, LEVELS, COLS), F32),
        ],
        scalars,
        lateral_velocity_components,
    )

    def tables(columns):
        return [
            pltpu.VMEM((56, LANES), F32),
            pltpu.VMEM((56, LANES), F32),
            pltpu.VMEM((56, columns), F32),
            pltpu.VMEM((columns // LANES, 8 * LEVELS, LANES), F32),
        ]

    sent = call(next_kernel, message, [], *blocks, after=(ratio, *exts[1:]))
    blocks.append(lax.ppermute(sent, AXES, SWAPS[2]))
    heat = call(
        home_kernel,
        field,
        [pltpu.VMEM((LEVELS, COLS), F32), *tables(COLS)],
        *exts, thermal_state, moisture_content, scalars,
        after=(sent,),
    )
    sent = call(next_kernel, message, [], *blocks, after=(heat,))
    blocks.append(lax.ppermute(sent, AXES, SWAPS[1]))
    tend0, average, correct = call(
        solve_kernel,
        [shape(2, LEVELS, COLS), shape(LEVELS, LANES), shape(LANES, COLS, dtype=BF16)],
        [pltpu.VMEM((2, LEVELS, COLS), F32)],
        thermal_state, moisture_content, heat, inverse, down, ratio, tend_late, scalars,
        after=(sent,),
    )
    off = lax.ppermute(average, AXES, OFF_CHIP)
    sent = call(last_kernel, shape(8, WIDE + LEVELS * 16), [], *blocks, average)
    last = lax.ppermute(sent, AXES, SWAPS[0])
    span_heating, token = call(
        span_kernel,
        [shape(LEVELS, 256), shape(8, LANES)],
        [pltpu.VMEM((80, 256), F32), pltpu.VMEM((LEVELS, 256), F32), *tables(256)],
        *exts, *blocks, last,
    )
    tendency_out = call(
        finish_kernel, shape(4, LEVELS, COLS),
        [pltpu.VMEM((4, LEVELS, COLS), F32), pltpu.SemaphoreType.DMA((4,))],
        tend0, tend_late, average, last, off, correct,
        after=(token,),
        hbm_out=True,
    )
    return tendency_out, span_heating


def solution(mesh):
    return jax.shard_map(
        shards,
        mesh=mesh,
        in_specs=(
            P(None, "elem"),
            P(None, "elem"),
            P(None, None, "elem"),
            P("elem"),
            P("elem"),
            P("elem"),
            P("elem"),
            P("elem", None),
            P("elem", None),
            P("gpt", None),
            P("gpt"),
        ),
        out_specs=(P(None, None, "elem"), P(None, ("elem", "gpt"))),
        check_vma=False,
    )
```
